128 devices in a mesh: row: 8 (over y, core), col: 16 (over z, x).
Axes of the slice: x: 4, y: 4, z: 4, core: 2. Of those that a mesh axis runs over, the one named last changes fastest.
Arguments:
- hamiltonian: bfloat16 [2048, 200704], P('row', 'col'), may hold values from -0.0546875 to 0.0546875
- term_now: bfloat16 [100352, 4096], P('row', 'col'), may hold values from -6 to 6
- hamiltonian_ids: int32 [8, 16, 78], P('row', 'col'), may hold values from 0 to 196, as said below
- term_ids: int32 [8, 16, 78], P('row', 'col'), may hold values from 0 to 196, as said below
- product_filter: int32 [4, 16, 32], P(None, 'row', 'col'), may hold values 0 or 1
- term_before: bfloat16 [2048, 4096], P('row', 'col'), may hold values from -6 to 6
- density_in: float32 [2048, 4096], P('row', 'col'), may hold values from -6 to 6
- coefficient: float32 [1], replicated, may hold values from 0.5 to 1.5
Outputs:
- term_next: bfloat16 [2048, 4096], P('row', 'col')
- density_out: float32 [2048, 4096], P('row', 'col')
The draws below stay inside these ranges and needn't reach their ends.
Inputs may be any that keep to these rules, and one draw needn't show every extreme that they name: `hamiltonian_ids`: in each cell's list the first entries are distinct block positions below 196 and the remaining entries equal 196, meaning no block; each list stores at most 78 blocks, and some list stores exactly 78. `term_ids`: likewise for the term's panels.
All inputs are finite; a program needn't handle non-finite values. No bound on the sum of `product_filter` on one device may be relied on, other than what follows from the above.
Results may differ from the reference program's by a relative error of at most 0.006.
Values may be sent and summed in bfloat16 or wider, within the bound.
No kernel may reach another device: no remote copies, remote signals or barrier semaphores. Data moves between devices by JAX's collectives and lax.ppermute only.
A program may use at most 128 MiB of HBM per device.

```python
import jax
import jax.numpy as jnp
from jax import lax

BS = 128
KB = 98
WB = 2
STEPS = 4
MAXB = 78
ROWS = 2048
COLS = 4096
HCOLS = 200704
TROWS = 100352
GBR = 16
GBC = 32
N_ROW = 8
N_COL = 16


def occupancy_lists(key):
    count_cells = N_ROW * N_COL
    first, second, third = jax.random.split(key, 3)
    lowest = max(MAXB // 3, 1)
    counts = jax.random.randint(first, (count_cells,), lowest, MAXB + 1)
    heavy = jax.random.randint(second, (), 0, count_cells)
    counts = jnp.where(jnp.arange(count_cells) == heavy, MAXB, counts)
    cell_keys = jax.random.split(third, count_cells)
    orders = jax.vmap(lambda k: jax.random.permutation(k, WB * KB))(cell_keys)[:, :MAXB]
    slots = jnp.arange(MAXB)[None, :]
    lists = jnp.where(slots < counts[:, None], orders, WB * KB)
    return lists.reshape(N_ROW, N_COL, MAXB).astype(jnp.int32)


def draw_hamiltonian_ids(key, part):
    key = jax.random.fold_in(key, 11)
    return occupancy_lists(key)


def draw_term_ids(key, part):
    key = jax.random.fold_in(key, 23)
    return occupancy_lists(key)


def touch_ends(values, key, smallest, largest):
    spot = [jax.random.randint(jax.random.fold_in(key, axis), (), 0, length) for axis, length in enumerate(values.shape)]
    longest = values.shape.index(max(values.shape))
    neighbour = spot[:longest] + [(spot[longest] + 1) % values.shape[longest]] + spot[longest + 1:]
    return values.at[tuple(spot)].set(smallest).at[tuple(neighbour)].set(largest)


def block_scale(own_key, shape, pieces, smallest, high):
    loudness = 1.0
    for axis_at, blocks in pieces:
        draws = jax.random.uniform(jax.random.fold_in(jax.random.fold_in(own_key, 6), axis_at), (blocks,), jnp.float32, smallest / len(pieces), high / len(pieces))
        loudness = loudness * jnp.repeat(jnp.exp(draws), shape[axis_at] // blocks).reshape((-1,) + (1,) * (len(shape) - 1 - axis_at))
    return loudness


def normal_values(rng, shape, deviation, bound, pieces=(), held_as=jnp.bfloat16):
    factor_of = block_scale(rng, shape, pieces, -0.22, 0.18) if pieces else 1.0
    array = jax.random.normal(rng, shape, jnp.float32) * deviation * factor_of
    return jnp.minimum(jnp.maximum(array, -bound), bound).astype(held_as)


def setup_inputs(seed: int = 0) -> dict:
    splits = jax.random.split(jax.random.key(seed), 9)
    hamiltonian = normal_values(splits[0], (ROWS, HCOLS), (KB * BS) ** -0.5, 0.0546875, ((0, 8), (1, 16)))
    term_now = normal_values(splits[1], (TROWS, COLS), 1.0, 6.0, ((0, 8), (1, 16)))
    hamiltonian_ids = draw_hamiltonian_ids(jax.random.fold_in(splits[8], 71), 0)
    term_ids = draw_term_ids(jax.random.fold_in(splits[8], 71), 0)
    product_filter = touch_ends((jax.random.randint(splits[4], (STEPS, GBR, GBC), 0, 4) < 3).astype(jnp.int32), jax.random.fold_in(splits[4], 1), 0, 1)
    term_before = normal_values(splits[5], (ROWS, COLS), 1.0, 6.0, ((0, 8), (1, 16)))
    density_in = normal_values(splits[6], (ROWS, COLS), 1.0, 6.0, ((0, 8), (1, 16)), jnp.float32)
    coefficient = jnp.clip(jax.random.uniform(splits[7], (1,), jnp.float32, 0.5, 1.5), 0.5, 1.5)
    return dict(hamiltonian=hamiltonian, term_now=term_now, hamiltonian_ids=hamiltonian_ids, term_ids=term_ids, product_filter=product_filter, term_before=term_before, density_in=density_in, coefficient=coefficient)


def block_flags(block_list):
    positions = jnp.arange(WB * KB, dtype=jnp.int32)
    return jnp.any(block_list[..., :, None] == positions, axis=-2)


def masked_left(panel, flags):
    blocks = panel.reshape(WB, BS, KB, BS)
    keep = flags.reshape(WB, 1, KB, 1)
    return jnp.where(keep, blocks, jnp.zeros((), panel.dtype)).reshape(WB * BS, KB * BS)


def masked_right(panel, flags):
    blocks = panel.reshape(KB, BS, WB, BS)
    keep = flags.reshape(KB, 1, WB, 1)
    return jnp.where(keep, blocks, jnp.zeros((), panel.dtype)).reshape(KB * BS, WB * BS)


def cell_product(left_panel, left_flags, right_panel, right_flags, filt):
    left_side = masked_left(left_panel, left_flags).astype(jnp.float32)
    right_side = masked_right(right_panel, right_flags).astype(jnp.float32)
    result = jnp.dot(left_side, right_side, precision=lax.Precision.HIGHEST).reshape(WB, BS, WB, BS)
    keep = filt.reshape(WB, 1, WB, 1) == 1
    return jnp.where(keep, result, jnp.zeros((), jnp.float32)).reshape(WB * BS, WB * BS)


def reference(hamiltonian, term_now, hamiltonian_ids, term_ids, product_filter, term_before, density_in, coefficient):
    left_flags_all = block_flags(hamiltonian_ids)
    right_flags_all = block_flags(term_ids)
    height = WB * BS
    inner = KB * BS

    def one_row(row_index):
        total = jnp.zeros((N_COL, height, height), jnp.float32)
        left_rows = lax.dynamic_slice_in_dim(hamiltonian, row_index * height, height, 0)
        for step in range(STEPS):
            rolled = jnp.roll(left_rows, step * inner, axis=1).reshape(height, N_COL, inner).transpose(1, 0, 2)
            left_flags = jnp.roll(left_flags_all[row_index], step, axis=0)
            source = ((row_index - step) % N_ROW).astype(jnp.int32)
            right_rows = lax.dynamic_slice_in_dim(term_now, source * inner, inner, 0)
            right_rows = right_rows.reshape(inner, N_COL, height).transpose(1, 0, 2)
            right_flags = right_flags_all[source]
            filt = lax.dynamic_slice_in_dim(product_filter[step], row_index * WB, WB, 0)
            filt = filt.reshape(WB, N_COL, WB).transpose(1, 0, 2)
            total = total + jax.vmap(cell_product)(rolled, left_flags, right_rows, right_flags, filt)
        return total.transpose(1, 0, 2).reshape(height, N_COL * height)

    product = lax.map(one_row, jnp.arange(N_ROW, dtype=jnp.int32)).reshape(N_ROW * height, N_COL * height)
    term_next = (2.0 * product - term_before.astype(jnp.float32)).astype(jnp.bfloat16)
    density_out = density_in + coefficient[0] * term_next.astype(jnp.float32)
    return term_next, density_out
```

```python
import functools

import jax
import jax.numpy as jnp
from jax import lax
from jax.experimental import pallas as pl
from jax.experimental.pallas import tpu as pltpu
from jax.sharding import PartitionSpec as P

BS = 128
KB = 98
WB = 2
STEPS = 4
MAXB = 78
N_ROW = 8
N_COL = 16
AXES = ("row", "col")
GROUP = 4
LISTED = 100
ZERO = 4 * MAXB


def left_near(i, j):
    if i % 2 == 1:
        return i - 1, j + 1
    return i - 1, j + 3 if j % 4 == 0 else j - 1


def right_near(i, j):
    if i % 2 == 1:
        return i + 1, j - 1
    return i + 1, j + 1 if j % 4 == 2 else j - 3


def left_far(i, j):
    if i % 2 == 1:
        return i - 2, j + 4 if j % 4 == 3 else j
    return None


def right_far(i, j):
    if i % 2 == 1:
        return i + 2, j if j % 4 == 3 else j - 4
    return None


def home_two(i, j):
    if i % 2 == 1:
        return i + 1, j - 1 if j % 4 == 3 else j + 3
    return i + 1, j + 1


def home_three(i, j):
    if i % 2 == 1:
        return i + 2, j - 1 if j % 4 == 3 else j + 3
    return i, j + 1


def home_one(i, j):
    if i % 2 == 1:
        return i + 1, j if j % 4 == 3 else j + 4
    return i + 1, j


def move(value, target):
    pairs = []
    for i in range(N_ROW):
        for j in range(N_COL):
            to = target(i, j)
            if to is not None:
                pairs.append((i * N_COL + j, (to[0] % N_ROW) * N_COL + to[1] % N_COL))
    return lax.ppermute(value, AXES, pairs)


def sources(target):
    found = [0] * (N_ROW * N_COL)
    for i in range(N_ROW):
        for j in range(N_COL):
            to = target(i, j)
            if to is not None:
                found[(to[0] % N_ROW) * N_COL + to[1] % N_COL] = i * N_COL + j
    return found


def gather_blocks_kernel(by_rows, ids_ref, panel_ref, out_ref, sem):
    def start(n, carry):
        place = jnp.minimum(ids_ref[n], WB * KB - 1)
        if by_rows:
            r, k = place // KB, place % KB
        else:
            r, k = place // WB, place % WB
        pltpu.make_async_copy(
            panel_ref.at[
                pl.ds(pl.multiple_of(r * BS, BS), BS), pl.ds(pl.multiple_of(k * BS, BS), BS)
            ],
            out_ref.at[pl.ds(pl.multiple_of(n * BS, BS), BS), :],
            sem,
        ).start()
        return carry

    lax.fori_loop(0, MAXB, start, 0)
    pltpu.make_async_copy(out_ref, out_ref, sem).wait()


def gather_blocks(panel, ids, by_rows):
    return pl.pallas_call(
        functools.partial(gather_blocks_kernel, by_rows),
        out_shape=jax.ShapeDtypeStruct((MAXB * BS, BS), panel.dtype),
        in_specs=[
            pl.BlockSpec(memory_space=pltpu.SMEM),
            pl.BlockSpec(memory_space=pl.ANY),
        ],
        out_specs=pl.BlockSpec(memory_space=pl.ANY),
        scratch_shapes=[pltpu.SemaphoreType.DMA],
        cost_estimate=pl.CostEstimate(
            flops=0, bytes_accessed=2 * MAXB * BS * BS * 2, transcendentals=0
        ),
    )(ids, panel)


def slots_of(ids, base):
    positions = jnp.arange(WB * KB, dtype=jnp.int32)
    hit = ids[:, None] == positions[None, :]
    slot = jnp.min(jnp.where(hit, jnp.arange(MAXB, dtype=jnp.int32)[:, None], MAXB), axis=0)
    return jnp.where(slot == MAXB, ZERO, slot + base)


def matched(left_slots, right_slots):
    left = left_slots.reshape(WB, KB)
    right = right_slots.reshape(KB, WB).T
    both = jnp.any(left != ZERO, axis=0) & jnp.any(right != ZERO, axis=0)
    inner = jnp.arange(KB, dtype=jnp.int32)
    rank = jnp.sum(both[:, None] & (inner[:, None] < inner[None, :]), axis=0)
    chosen = both[:, None] & (rank[:, None] == jnp.arange(LISTED, dtype=jnp.int32)[None, :])
    four = jnp.concatenate([left, right], axis=0)
    listed = ZERO + jnp.sum(jnp.where(chosen[None], four[:, :, None] - ZERO, 0), axis=1)
    count = jnp.sum(both.astype(jnp.int32))
    return listed, (count + GROUP - 1) // GROUP


def multiply(listed_ref, count_ref, product, held, out_ref):
    def block(which, at):
        slot = listed_ref[product, which, at]
        return held[pl.ds(pl.multiple_of(slot * BS, BS), BS), :]

    out_ref[product] = jnp.zeros((WB * BS, WB * BS), jnp.float32)

    def step(t, carry):
        ks = [t * GROUP + q for q in range(GROUP)]
        left = jnp.concatenate(
            [jnp.concatenate([block(r, k) for k in ks], axis=1) for r in range(WB)], axis=0
        )
        right = jnp.concatenate(
            [jnp.concatenate([block(WB + c, k) for k in ks], axis=0) for c in range(WB)], axis=1
        )
        out_ref[product] += jnp.dot(left, right, preferred_element_type=jnp.float32)
        return carry

    lax.fori_loop(0, count_ref[product], step, 0)


def own_kernel(listed_ref, count_ref, left_ref, right_ref, out_ref, held, sems):
    size = MAXB * BS
    held[pl.ds(ZERO * BS, BS), :] = jnp.zeros((BS, BS), held.dtype)
    copies = [
        pltpu.make_async_copy(ref, held.at[pl.ds(n * size, size), :], sems.at[n])
        for n, ref in ((0, left_ref), (2, right_ref))
    ]
    for copy in copies:
        copy.start()
    for copy in copies:
        copy.wait()
    multiply(listed_ref, count_ref, 0, held, out_ref)


def products_kernel(
    odd_ref,
    listed_ref,
    count_ref,
    left_own_ref,
    right_own_ref,
    left_near_ref,
    right_near_ref,
    left_far_ref,
    right_far_ref,
    out_ref,
    held,
    sems,
):
    size = MAXB * BS

    def load(refs):
        for n, ref in enumerate(refs):
            pltpu.make_async_copy(ref, held.at[pl.ds(n * size, size), :], sems.at[n]).start()

    @pl.when(odd_ref[0] == 1)
    def _():
        load((left_far_ref, left_near_ref, right_near_ref, right_far_ref))

    @pl.when(odd_ref[0] == 0)
    def _():
        load((left_near_ref, left_own_ref, right_own_ref, right_near_ref))

    held[pl.ds(ZERO * BS, BS), :] = jnp.zeros((BS, BS), held.dtype)
    for n in range(4):
        part = held.at[pl.ds(n * size, size), :]
        pltpu.make_async_copy(part, part, sems.at[n]).wait()
    for product in range(3):
        multiply(listed_ref, count_ref, product, held, out_ref)


def run_products(kernel, scalars, panels, count):
    return pl.pallas_call(
        kernel,
        out_shape=jax.ShapeDtypeStruct((count, WB * BS, WB * BS), jnp.float32),
        in_specs=[pl.BlockSpec(memory_space=pltpu.SMEM)] * len(scalars)
        + [pl.BlockSpec(memory_space=pl.ANY)] * len(panels),
        out_specs=pl.BlockSpec(memory_space=pltpu.VMEM),
        scratch_shapes=[
            pltpu.VMEM(((ZERO + 1) * BS, BS), jnp.bfloat16),
            pltpu.SemaphoreType.DMA((4,)),
        ],
        compiler_params=pltpu.CompilerParams(vmem_limit_bytes=32 * 1024 * 1024),
        cost_estimate=pl.CostEstimate(
            flops=count * 2 * WB * WB * BS * BS * BS * 40,
            bytes_accessed=len(panels) * MAXB * BS * BS * 2,
            transcendentals=0,
        ),
    )(*scalars, *panels)


def per_device(
    hamiltonian,
    term_now,
    hamiltonian_ids,
    term_ids,
    product_filter,
    term_before,
    density_in,
    coefficient,
):
    left_ids = hamiltonian_ids.reshape(-1)
    right_ids = term_ids.reshape(-1)
    all_ids = lax.all_gather(jnp.stack([left_ids, right_ids]), AXES)

    left_own = gather_blocks(hamiltonian, left_ids, True)
    left_n = move(left_own, left_near)
    left_f = move(left_own, left_far)
    right_own = gather_blocks(term_now, right_ids, False)
    right_n = move(right_own, right_near)
    right_f = move(right_own, right_far)

    me = lax.axis_index("row") * N_COL + lax.axis_index("col")
    odd = lax.axis_index("row") % 2

    def ids_from(target, side):
        return all_ids[jnp.asarray(sources(target), jnp.int32)[me], side]

    near_l, near_r = ids_from(left_near, 0), ids_from(right_near, 1)
    far_l, far_r = ids_from(left_far, 0), ids_from(right_far, 1)
    is_odd = odd == 1
    l1 = slots_of(jnp.where(is_odd, far_l, near_l), 0)
    l2 = slots_of(jnp.where(is_odd, near_l, left_ids), MAXB)
    r1 = slots_of(jnp.where(is_odd, near_r, right_ids), 2 * MAXB)
    r2 = slots_of(jnp.where(is_odd, far_r, near_r), 3 * MAXB)
    lists = [
        matched(jnp.where(is_odd, l2, l1), jnp.where(is_odd, r1, r2)),
        matched(jnp.where(is_odd, l1, l2), jnp.where(is_odd, r1, r2)),
        matched(jnp.where(is_odd, l2, l1), jnp.where(is_odd, r2, r1)),
    ]
    listed = jnp.stack([entry[0] for entry in lists])
    counts = jnp.stack([entry[1] for entry in lists])
    own_listed, own_count = matched(slots_of(left_ids, 0), slots_of(right_ids, 2 * MAXB))

    own = run_products(
        own_kernel, (own_listed[None], own_count[None]), (left_own, right_own), 1
    )
    results = run_products(
        products_kernel,
        (odd.astype(jnp.int32)[None], listed, counts),
        (left_own, right_own, left_n, right_n, left_f, right_f),
        3,
    )
    home = [
        move(results[0], home_two),
        move(results[1], home_three),
        move(results[2], home_one),
    ]
    height = WB * BS

    def kept(result, filt):
        keep = filt.reshape(WB, 1, WB, 1) == 1
        return jnp.where(keep, result.reshape(WB, BS, WB, BS), 0.0).reshape(height, height)

    third = jnp.where(is_odd, product_filter[3], product_filter[1])
    first = jnp.where(is_odd, product_filter[1], product_filter[3])
    total = (
        kept(own[0], product_filter[0])
        + kept(home[0], product_filter[2])
        + kept(home[1], third)
        + kept(home[2], first)
    )
    term_next = (2.0 * total - term_before.astype(jnp.float32)).astype(jnp.bfloat16)
    density_out = density_in + coefficient[0] * term_next.astype(jnp.float32)
    return (term_next, density_out)


def solution(mesh):
    return jax.shard_map(
        per_device,
        mesh=mesh,
        in_specs=(
            P("row", "col"),
            P("row", "col"),
            P("row", "col", None),
            P("row", "col", None),
            P(None, "row", "col"),
            P("row", "col"),
            P("row", "col"),
            P(),
        ),
        out_specs=(P("row", "col"), P("row", "col")),
        check_vma=False,
    )
```

```python
import functools

import jax
import jax.numpy as jnp
from jax import lax
from jax.experimental import pallas as pl
from jax.experimental.pallas import tpu as pltpu
from jax.sharding import PartitionSpec as P

BS = 128
KB = 98
WB = 2
STEPS = 4
MAXB = 78
N_ROW = 8
N_COL = 16
AXES = ("row", "col")
GROUP = 8
LANES = 128
KERNEL_VMEM = 8 * 1024 * 1024
STORED = MAXB * BS
TABLE_AT = STORED + BS
TABLE = 16
PACKED = TABLE_AT + TABLE


def left_near(i, j):
    if i % 2 == 1:
        return i - 1, j + 1
    return i - 1, j + 3 if j % 4 == 0 else j - 1


def right_near(i, j):
    if i % 2 == 1:
        return i + 1, j - 1
    return i + 1, j + 1 if j % 4 == 2 else j - 3


def left_far(i, j):
    if i % 2 == 1:
        return i - 2, j + 4 if j % 4 == 3 else j
    return None


def right_far(i, j):
    if i % 2 == 1:
        return i + 2, j if j % 4 == 3 else j - 4
    return None


def home_two(i, j):
    if i % 2 == 1:
        return i + 1, j - 1 if j % 4 == 3 else j + 3
    return i + 1, j + 1


def home_three(i, j):
    if i % 2 == 1:
        return i + 2, j - 1 if j % 4 == 3 else j + 3
    return i, j + 1


def home_one(i, j):
    if i % 2 == 1:
        return i + 1, j if j % 4 == 3 else j + 4
    return i + 1, j


def move(value, target):
    pairs = []
    for i in range(N_ROW):
        for j in range(N_COL):
            to = target(i, j)
            if to is not None:
                pairs.append((i * N_COL + j, (to[0] % N_ROW) * N_COL + to[1] % N_COL))
    return lax.ppermute(value, AXES, pairs)


def gather_blocks_kernel(
    left_ids_ref, right_ids_ref, left_ref, right_ref, left_out, right_out, left_ids, right_ids, id_sems, sems
):
    id_copies = [
        pltpu.make_async_copy(source, target, id_sems.at[n])
        for n, (source, target) in enumerate(
            ((left_ids_ref, left_ids), (right_ids_ref, right_ids))
        )
    ]
    for copy in id_copies:
        copy.start()
    row = lax.broadcasted_iota(jnp.int32, (8, LANES), 0)
    lane = lax.broadcasted_iota(jnp.int32, (8, LANES), 1)
    sides = ((left_ids, left_ref, left_out, KB), (right_ids, right_ref, right_out, WB))
    tables = []
    for side, (ids, panel_ref, out_ref, across) in enumerate(sides):
        id_copies[side].wait()

        def start(n, table):
            place = ids[0, 0, n]
            r, k = place // across, place % across
            pltpu.make_async_copy(
                panel_ref.at[
                    pl.ds(pl.multiple_of(jnp.minimum(r, WB * KB // across - 1) * BS, BS), BS),
                    pl.ds(pl.multiple_of(k * BS, BS), BS),
                ],
                out_ref.at[pl.ds(pl.multiple_of(n * BS, BS), BS), :],
                sems.at[side],
            ).start()
            outer, inner = (r, k) if across == KB else (k, r)
            return jnp.where((row == outer) & (lane == inner), n, table)

        tables.append(
            lax.fori_loop(0, MAXB, start, jnp.full((8, LANES), MAXB, jnp.int32), unroll=13)
        )
    for (_, _, out_ref, _), table in zip(sides, tables):
        out_ref[pl.ds(STORED, BS), :] = jnp.zeros((BS, BS), out_ref.dtype)
        both = jnp.concatenate([table, table], axis=0).astype(jnp.float32)
        out_ref[pl.ds(TABLE_AT, TABLE), :] = both.astype(out_ref.dtype)
    for side, (_, _, out_ref, _) in enumerate(sides):
        blocks = out_ref.at[pl.ds(0, STORED), :]
        pltpu.make_async_copy(blocks, blocks, sems.at[side]).wait()


def gather_blocks(left, right, left_ids, right_ids):
    any_space = pl.BlockSpec(memory_space=pl.ANY)
    return pl.pallas_call(
        gather_blocks_kernel,
        out_shape=[pltpu.VMEM((PACKED, BS), left.dtype)] * 2,
        in_specs=[any_space] * 4,
        out_specs=[pl.BlockSpec(memory_space=pltpu.VMEM)] * 2,
        scratch_shapes=[
            pltpu.SMEM(left_ids.shape, jnp.int32),
            pltpu.SMEM(right_ids.shape, jnp.int32),
            pltpu.SemaphoreType.DMA((2,)),
            pltpu.SemaphoreType.DMA((2,)),
        ],
        compiler_params=pltpu.CompilerParams(vmem_limit_bytes=KERNEL_VMEM),
        cost_estimate=pl.CostEstimate(
            flops=0, bytes_accessed=4 * PACKED * BS * 2, transcendentals=0
        ),
    )(
        left_ids,
        right_ids,
        pltpu.with_memory_space_constraint(left, pltpu.HBM),
        pltpu.with_memory_space_constraint(right, pltpu.HBM),
    )


def slot_words(left, right):
    both = (jnp.minimum(left[0:1], left[1:2]) < MAXB) & (jnp.minimum(right[0:1], right[1:2]) < MAXB)
    slots = (left[0:1], left[1:2], right[0:1], right[1:2])
    word = sum(slot << (8 * n) for n, slot in enumerate(slots))
    return jnp.where(both, word, -1)


def multiply(left_ref, right_ref, words, chosen, out_ref):
    def choose(k, count):
        word = words[k]
        chosen[count] = word
        return count + (word >= 0).astype(jnp.int32)

    count = lax.fori_loop(0, KB, choose, 0, unroll=14)
    nothing = MAXB * 0x01010101
    for q in range(GROUP - 1):
        chosen[count + q] = nothing
    out_ref[...] = jnp.zeros(out_ref.shape, out_ref.dtype)

    def block(ref, word, n):
        slot = lax.shift_right_logical(word, 8 * n) & 0xFF
        return ref[pl.ds(pl.multiple_of(slot * BS, BS), BS), :]

    def step(t, carry):
        words = [chosen[t * GROUP + q] for q in range(GROUP)]
        left = jnp.concatenate(
            [
                jnp.concatenate([block(left_ref, word, r) for word in words], axis=1)
                for r in range(WB)
            ],
            axis=0,
        )
        right = jnp.concatenate(
            [
                jnp.concatenate([block(right_ref, word, WB + c) for word in words], axis=0)
                for c in range(WB)
            ],
            axis=1,
        )
        out_ref[...] += jnp.dot(left, right, preferred_element_type=jnp.float32)
        return carry

    lax.fori_loop(0, (count + GROUP - 1) // GROUP, step, 0)


def table_in(ref):
    return ref[pl.ds(TABLE_AT, TABLE), :].astype(jnp.float32).astype(jnp.int32)


def to_scalars(rows, held, words, sem):
    rows = rows + [rows[0]] * (8 - len(rows))
    held[...] = jnp.concatenate(rows, axis=0)
    copy = pltpu.make_async_copy(held, words, sem)
    copy.start()
    copy.wait()


def masked(filter_ref, step, value):
    rows = []
    for r in range(WB):
        row = []
        for c in range(WB):
            block = value[r * BS : (r + 1) * BS, c * BS : (c + 1) * BS]
            row.append(jnp.where(filter_ref[step, r, c] == 1, block, 0.0))
        rows.append(jnp.concatenate(row, axis=1))
    return jnp.concatenate(rows, axis=0)


def base_kernel(filter_ref, left_ref, right_ref, before_ref, out_ref, product, held, words, chosen, sem):
    to_scalars([slot_words(table_in(left_ref), table_in(right_ref))], held, words, sem)
    multiply(left_ref, right_ref, words.at[0], chosen, product)
    out_ref[...] = 2.0 * masked(filter_ref, 0, product[...]) - before_ref[...].astype(jnp.float32)


def products_kernel(
    left_near_ref,
    right_near_ref,
    left_far_ref,
    right_far_ref,
    left_own_ref,
    right_own_ref,
    two_ref,
    three_ref,
    one_ref,
    held,
    words,
    chosen,
    sem,
):
    odd = lax.axis_index("row") % 2 == 1
    left_near, right_near = table_in(left_near_ref), table_in(right_near_ref)
    left_other = jnp.where(odd, table_in(left_far_ref), table_in(left_own_ref))
    right_other = jnp.where(odd, table_in(right_far_ref), table_in(right_own_ref))
    to_scalars(
        [
            slot_words(left_near, right_near),
            slot_words(left_other, right_near),
            slot_words(left_near, right_other),
        ],
        held,
        words,
        sem,
    )
    multiply(left_near_ref, right_near_ref, words.at[0], chosen, two_ref)

    @pl.when(odd)
    def _():
        multiply(left_far_ref, right_near_ref, words.at[1], chosen, three_ref)
        multiply(left_near_ref, right_far_ref, words.at[2], chosen, one_ref)

    @pl.when(jnp.logical_not(odd))
    def _():
        multiply(left_own_ref, right_near_ref, words.at[1], chosen, three_ref)
        multiply(left_near_ref, right_own_ref, words.at[2], chosen, one_ref)


def final_kernel(
    filter_ref, coefficient_ref, base_ref, two_ref, three_ref, one_ref, density_ref, term_out, density_out
):
    odd = lax.axis_index("row") % 2
    total = (
        masked(filter_ref, 2, two_ref[...])
        + masked(filter_ref, 1 + 2 * odd, three_ref[...])
        + masked(filter_ref, 3 - 2 * odd, one_ref[...])
    )
    term_next = (2.0 * total + base_ref[...]).astype(jnp.bfloat16)
    term_out[...] = term_next
    density_out[...] = density_ref[...] + coefficient_ref[0] * term_next.astype(jnp.float32)


IN_VMEM = pl.BlockSpec(memory_space=pltpu.VMEM)
IN_SMEM = pl.BlockSpec(memory_space=pltpu.SMEM)
PANEL = (WB * BS, WB * BS)
RESULT = jax.ShapeDtypeStruct(PANEL, jnp.float32)
LISTS = [
    pltpu.VMEM((8, LANES), jnp.int32),
    pltpu.SMEM((8, LANES), jnp.int32),
    pltpu.SMEM((LANES,), jnp.int32),
    pltpu.SemaphoreType.DMA,
]


def run_kernel(kernel, in_specs, out_shape, scratch_shapes, products, *args):
    return pl.pallas_call(
        kernel,
        out_shape=out_shape,
        in_specs=in_specs,
        out_specs=[IN_VMEM] * len(out_shape),
        scratch_shapes=scratch_shapes,
        compiler_params=pltpu.CompilerParams(vmem_limit_bytes=KERNEL_VMEM),
        cost_estimate=pl.CostEstimate(
            flops=products * 2 * WB * WB * BS * BS * BS * 40,
            bytes_accessed=4 * len(out_shape) * WB * WB * BS * BS,
            transcendentals=0,
        ),
    )(*args)


def per_device(
    hamiltonian,
    term_now,
    hamiltonian_ids,
    term_ids,
    product_filter,
    term_before,
    density_in,
    coefficient,
):
    left_own, right_own = gather_blocks(hamiltonian, term_now, hamiltonian_ids, term_ids)
    left_n = move(left_own, left_near)
    right_n = move(right_own, right_near)
    left_f = move(left_own, left_far)
    right_f = move(right_own, right_far)

    def in_vmem(panel):
        return pltpu.with_memory_space_constraint(panel, pltpu.VMEM)

    two, three, one = run_kernel(
        products_kernel,
        [IN_VMEM] * 6,
        [RESULT] * 3,
        LISTS,
        3,
        *[in_vmem(panel) for panel in (left_n, right_n, left_f, right_f, left_own, right_own)],
    )
    two, three, one = move(two, home_two), move(three, home_three), move(one, home_one)
    (base,) = run_kernel(
        base_kernel,
        [IN_SMEM] + [IN_VMEM] * 3,
        [RESULT],
        [pltpu.VMEM(PANEL, jnp.float32)] + LISTS,
        1,
        product_filter,
        in_vmem(left_own),
        in_vmem(right_own),
        term_before,
    )
    term_next, density_out = run_kernel(
        final_kernel,
        [IN_SMEM] * 2 + [IN_VMEM] * 5,
        [
            jax.ShapeDtypeStruct(term_before.shape, jnp.bfloat16),
            jax.ShapeDtypeStruct(density_in.shape, jnp.float32),
        ],
        [],
        0,
        product_filter,
        coefficient,
        base,
        two,
        three,
        one,
        density_in,
    )
    return (term_next, density_out)


def solution(mesh):
    return jax.shard_map(
        per_device,
        mesh=mesh,
        in_specs=(
            P("row", "col"),
            P("row", "col"),
            P("row", "col", None),
            P("row", "col", None),
            P(None, "row", "col"),
            P("row", "col"),
            P("row", "col"),
            P(),
        ),
        out_specs=(P("row", "col"), P("row", "col")),
        check_vma=False,
    )
```

```python
import functools

import jax
import jax.numpy as jnp
from jax import lax
from jax.experimental import pallas as pl
from jax.experimental.pallas import tpu as pltpu
from jax.sharding import PartitionSpec as P

BS = 128
KB = 98
WB = 2
STEPS = 4
MAXB = 78
N_ROW = 8
N_COL = 16
AXES = ("row", "col")
GROUP = 16
LANES = 128
KERNEL_VMEM = 8 * 1024 * 1024
STORED = MAXB * BS
TABLE_AT = STORED + BS
TABLE = 16
PACKED = TABLE_AT + TABLE


def left_near(i, j):
    if i % 2 == 1:
        return i - 1, j + 1
    return i - 1, j - 1 if j % 4 == 1 else j + 3


def right_near(i, j):
    if i % 2 == 1:
        return i + 1, j - 1
    return i + 1, j - 3 if j % 4 == 3 else j + 1


def left_far(i, j):
    if i % 2 == 1:
        return i - 2, j if j % 4 == 0 else j + 4
    return None


def right_far(i, j):
    if i % 2 == 1:
        return i + 2, j - 4 if j % 4 == 0 else j
    return None


def home_two(i, j):
    if i % 2 == 1:
        return i + 1, j + 3 if j % 4 == 0 else j - 1
    return i + 1, j + 1


def home_three(i, j):
    if i % 2 == 1:
        return i + 2, j + 3 if j % 4 == 0 else j - 1
    return i, j + 1


def home_one(i, j):
    if i % 2 == 1:
        return i + 1, j + 4 if j % 4 == 0 else j
    return i + 1, j


def move(value, target):
    pairs = []
    for i in range(N_ROW):
        for j in range(N_COL):
            to = target(i, j)
            if to is not None:
                pairs.append((i * N_COL + j, (to[0] % N_ROW) * N_COL + to[1] % N_COL))
    return lax.ppermute(value, AXES, pairs)


def gather_blocks_kernel(
    left_ids_ref, right_ids_ref, left_ref, right_ref, left_out, right_out, left_ids, right_ids, id_sems, sems
):
    id_copies = [
        pltpu.make_async_copy(source, target, id_sems.at[n])
        for n, (source, target) in enumerate(
            ((left_ids_ref, left_ids), (right_ids_ref, right_ids))
        )
    ]
    for copy in id_copies:
        copy.start()
    row = lax.broadcasted_iota(jnp.int32, (8, LANES), 0)
    lane = lax.broadcasted_iota(jnp.int32, (8, LANES), 1)
    sides = ((left_ids, left_ref, left_out, KB), (right_ids, right_ref, right_out, WB))
    tables = []
    for side, (ids, panel_ref, out_ref, across) in enumerate(sides):
        id_copies[side].wait()

        def start(n, table):
            place = ids[0, 0, n]
            r, k = place // across, place % across
            read = jnp.where(place < WB * KB, place, n)
            pltpu.make_async_copy(
                panel_ref.at[
                    pl.ds(pl.multiple_of(read // across * BS, BS), BS),
                    pl.ds(pl.multiple_of(read % across * BS, BS), BS),
                ],
                out_ref.at[pl.ds(pl.multiple_of(n * BS, BS), BS), :],
                sems.at[side],
            ).start()
            outer, inner = (r, k) if across == KB else (k, r)
            return jnp.where((row == outer) & (lane == inner), n, table)

        tables.append(
            lax.fori_loop(0, MAXB, start, jnp.full((8, LANES), MAXB, jnp.int32), unroll=13)
        )
    for (_, _, out_ref, _), table in zip(sides, tables):
        out_ref[pl.ds(STORED, BS), :] = jnp.zeros((BS, BS), out_ref.dtype)
        both = jnp.concatenate([table, table], axis=0).astype(jnp.float32)
        out_ref[pl.ds(TABLE_AT, TABLE), :] = both.astype(out_ref.dtype)
    for side, (_, _, out_ref, _) in enumerate(sides):
        blocks = out_ref.at[pl.ds(0, STORED), :]
        pltpu.make_async_copy(blocks, blocks, sems.at[side]).wait()


def gather_blocks(left, right, left_ids, right_ids):
    any_space = pl.BlockSpec(memory_space=pl.ANY)
    return pl.pallas_call(
        gather_blocks_kernel,
        out_shape=[pltpu.VMEM((PACKED, BS), left.dtype)] * 2,
        in_specs=[any_space] * 4,
        out_specs=[pl.BlockSpec(memory_space=pltpu.VMEM)] * 2,
        scratch_shapes=[
            pltpu.SMEM(left_ids.shape, jnp.int32),
            pltpu.SMEM(right_ids.shape, jnp.int32),
            pltpu.SemaphoreType.DMA((2,)),
            pltpu.SemaphoreType.DMA((2,)),
        ],
        compiler_params=pltpu.CompilerParams(vmem_limit_bytes=KERNEL_VMEM),
        cost_estimate=pl.CostEstimate(
            flops=0, bytes_accessed=4 * PACKED * BS * 2, transcendentals=0
        ),
    )(
        left_ids,
        right_ids,
        pltpu.with_memory_space_constraint(left, pltpu.HBM),
        pltpu.with_memory_space_constraint(right, pltpu.HBM),
    )


def slot_words(left, right):
    both = (jnp.minimum(left[0:1], left[1:2]) < MAXB) & (jnp.minimum(right[0:1], right[1:2]) < MAXB)
    slots = (left[0:1], left[1:2], right[0:1], right[1:2])
    word = sum(slot << (8 * n) for n, slot in enumerate(slots))
    return jnp.where(both, word, -1)


def multiply(left_ref, right_ref, words, chosen, out_ref):
    def choose(k, count):
        word = words[k]
        chosen[count] = word
        return count + (word >= 0).astype(jnp.int32)

    count = lax.fori_loop(0, KB, choose, 0, unroll=14)
    nothing = MAXB * 0x01010101
    for q in range(GROUP - 1):
        chosen[count + q] = nothing
    out_ref[...] = jnp.zeros(out_ref.shape, out_ref.dtype)

    def block(ref, word, n):
        slot = lax.shift_right_logical(word, 8 * n) & 0xFF
        return ref[pl.ds(pl.multiple_of(slot * BS, BS), BS), :]

    def step(t, carry):
        words = [chosen[t * GROUP + q] for q in range(GROUP)]
        left = jnp.concatenate(
            [
                jnp.concatenate([block(left_ref, word, r) for word in words], axis=1)
                for r in range(WB)
            ],
            axis=0,
        )
        right = jnp.concatenate(
            [
                jnp.concatenate([block(right_ref, word, WB + c) for word in words], axis=0)
                for c in range(WB)
            ],
            axis=1,
        )
        out_ref[...] += jnp.dot(left, right, preferred_element_type=jnp.float32)
        return carry

    lax.fori_loop(0, (count + GROUP - 1) // GROUP, step, 0)


def table_in(ref):
    return ref[pl.ds(TABLE_AT, TABLE), :].astype(jnp.float32).astype(jnp.int32)


def to_scalars(rows, held, words, sem):
    rows = rows + [rows[0]] * (8 - len(rows))
    held[...] = jnp.concatenate(rows, axis=0)
    copy = pltpu.make_async_copy(held, words, sem)
    copy.start()
    copy.wait()


def masked(filter_ref, step, value):
    rows = []
    for r in range(WB):
        row = []
        for c in range(WB):
            block = value[r * BS : (r + 1) * BS, c * BS : (c + 1) * BS]
            row.append(jnp.where(filter_ref[step, r, c] == 1, block, 0.0))
        rows.append(jnp.concatenate(row, axis=1))
    return jnp.concatenate(rows, axis=0)


def base_kernel(filter_ref, left_ref, right_ref, before_ref, out_ref, product, held, words, chosen, sem):
    to_scalars([slot_words(table_in(left_ref), table_in(right_ref))], held, words, sem)
    multiply(left_ref, right_ref, words.at[0], chosen, product)
    out_ref[...] = 2.0 * masked(filter_ref, 0, product[...]) - before_ref[...].astype(jnp.float32)


def send_product(left_ref, right_ref, words, chosen, product, out_ref):
    multiply(left_ref, right_ref, words, chosen, product)
    out_ref[...] = product[...].astype(out_ref.dtype)


def products_kernel(
    left_near_ref,
    right_near_ref,
    left_far_ref,
    right_far_ref,
    left_own_ref,
    right_own_ref,
    two_ref,
    three_ref,
    one_ref,
    product,
    held,
    words,
    chosen,
    sem,
):
    odd = lax.axis_index("row") % 2 == 1
    left_near, right_near = table_in(left_near_ref), table_in(right_near_ref)
    left_other = jnp.where(odd, table_in(left_far_ref), table_in(left_own_ref))
    right_other = jnp.where(odd, table_in(right_far_ref), table_in(right_own_ref))
    to_scalars(
        [
            slot_words(left_near, right_near),
            slot_words(left_other, right_near),
            slot_words(left_near, right_other),
        ],
        held,
        words,
        sem,
    )
    send_product(left_near_ref, right_near_ref, words.at[0], chosen, product, two_ref)

    @pl.when(odd)
    def _():
        send_product(left_far_ref, right_near_ref, words.at[1], chosen, product, three_ref)
        send_product(left_near_ref, right_far_ref, words.at[2], chosen, product, one_ref)

    @pl.when(jnp.logical_not(odd))
    def _():
        send_product(left_own_ref, right_near_ref, words.at[1], chosen, product, three_ref)
        send_product(left_near_ref, right_own_ref, words.at[2], chosen, product, one_ref)


def final_kernel(
    filter_ref, coefficient_ref, base_ref, two_ref, three_ref, one_ref, density_ref, term_out, density_out
):
    odd = lax.axis_index("row") % 2
    total = (
        masked(filter_ref, 2, two_ref[...].astype(jnp.float32))
        + masked(filter_ref, 1 + 2 * odd, three_ref[...].astype(jnp.float32))
        + masked(filter_ref, 3 - 2 * odd, one_ref[...].astype(jnp.float32))
    )
    term_next = (2.0 * total + base_ref[...]).astype(jnp.bfloat16)
    term_out[...] = term_next
    density_out[...] = density_ref[...] + coefficient_ref[0] * term_next.astype(jnp.float32)


IN_VMEM = pl.BlockSpec(memory_space=pltpu.VMEM)
IN_SMEM = pl.BlockSpec(memory_space=pltpu.SMEM)
PANEL = (WB * BS, WB * BS)
RESULT = jax.ShapeDtypeStruct(PANEL, jnp.float32)
LISTS = [
    pltpu.VMEM((8, LANES), jnp.int32),
    pltpu.SMEM((8, LANES), jnp.int32),
    pltpu.SMEM((LANES,), jnp.int32),
    pltpu.SemaphoreType.DMA,
]


def run_kernel(kernel, in_specs, out_shape, scratch_shapes, products, *args):
    return pl.pallas_call(
        kernel,
        out_shape=out_shape,
        in_specs=in_specs,
        out_specs=[IN_VMEM] * len(out_shape),
        scratch_shapes=scratch_shapes,
        compiler_params=pltpu.CompilerParams(vmem_limit_bytes=KERNEL_VMEM),
        cost_estimate=pl.CostEstimate(
            flops=products * 2 * WB * WB * BS * BS * BS * 40,
            bytes_accessed=4 * len(out_shape) * WB * WB * BS * BS,
            transcendentals=0,
        ),
    )(*args)


def per_device(
    hamiltonian,
    term_now,
    hamiltonian_ids,
    term_ids,
    product_filter,
    term_before,
    density_in,
    coefficient,
):
    left_own, right_own = gather_blocks(hamiltonian, term_now, hamiltonian_ids, term_ids)
    left_n = move(left_own, left_near)
    right_f = move(right_own, right_far)
    right_n = move(right_own, right_near)
    left_f = move(left_own, left_far)

    def in_vmem(panel):
        return pltpu.with_memory_space_constraint(panel, pltpu.VMEM)

    two, three, one = run_kernel(
        products_kernel,
        [IN_VMEM] * 6,
        [jax.ShapeDtypeStruct(PANEL, jnp.bfloat16)] * 3,
        [pltpu.VMEM(PANEL, jnp.float32)] + LISTS,
        3,
        *[in_vmem(panel) for panel in (left_n, right_n, left_f, right_f, left_own, right_own)],
    )
    two, three, one = move(two, home_two), move(three, home_three), move(one, home_one)
    (base,) = run_kernel(
        base_kernel,
        [IN_SMEM] + [IN_VMEM] * 3,
        [RESULT],
        [pltpu.VMEM(PANEL, jnp.float32)] + LISTS,
        1,
        product_filter,
        in_vmem(left_own),
        in_vmem(right_own),
        term_before,
    )
    term_next, density_out = run_kernel(
        final_kernel,
        [IN_SMEM] * 2 + [IN_VMEM] * 5,
        [
            jax.ShapeDtypeStruct(term_before.shape, jnp.bfloat16),
            jax.ShapeDtypeStruct(density_in.shape, jnp.float32),
        ],
        [],
        0,
        product_filter,
        coefficient,
        base,
        two,
        three,
        one,
        density_in,
    )
    return (term_next, density_out)


def solution(mesh):
    return jax.shard_map(
        per_device,
        mesh=mesh,
        in_specs=(
            P("row", "col"),
            P("row", "col"),
            P("row", "col", None),
            P("row", "col", None),
            P(None, "row", "col"),
            P("row", "col"),
            P("row", "col"),
            P(),
        ),
        out_specs=(P("row", "col"), P("row", "col")),
        check_vma=False,
    )
```

```python
import functools

import jax
import jax.numpy as jnp
from jax import lax
from jax.experimental import pallas as pl
from jax.experimental.pallas import tpu as pltpu
from jax.sharding import PartitionSpec as P

BS = 128
KB = 98
WB = 2
STEPS = 4
MAXB = 78
N_ROW = 8
N_COL = 16
AXES = ("row", "col")
GROUP = 16
LANES = 128
KERNEL_VMEM = 4 * 1024 * 1024
STORED = MAXB * BS
TABLE_AT = STORED + BS
TABLE = 16
PACKED = TABLE_AT + TABLE


def left_near(i, j):
    if i % 2 == 1:
        return i - 1, j + 1
    return i - 1, j - 1 if j % 4 == 1 else j + 3


def right_near(i, j):
    if i % 2 == 1:
        return i + 1, j - 1
    return i + 1, j - 3 if j % 4 == 3 else j + 1


def left_far(i, j):
    if i % 2 == 1:
        return i - 2, j if j % 4 == 0 else j + 4
    return None


def right_far(i, j):
    if i % 2 == 1:
        return i + 2, j - 4 if j % 4 == 0 else j
    return None


def home_two(i, j):
    if i % 2 == 1:
        return i + 1, j + 3 if j % 4 == 0 else j - 1
    return i + 1, j + 1


def home_three(i, j):
    if i % 2 == 1:
        return i + 2, j + 3 if j % 4 == 0 else j - 1
    return i, j + 1


def home_one(i, j):
    if i % 2 == 1:
        return i + 1, j + 4 if j % 4 == 0 else j
    return i + 1, j


def move(value, target):
    pairs = []
    for i in range(N_ROW):
        for j in range(N_COL):
            to = target(i, j)
            if to is not None:
                pairs.append((i * N_COL + j, (to[0] % N_ROW) * N_COL + to[1] % N_COL))
    return lax.ppermute(value, AXES, pairs)


def gather_blocks_kernel(across, ids_ref, panel_ref, out_ref, ids, id_sem, sem):
    id_copy = pltpu.make_async_copy(ids_ref, ids, id_sem)
    id_copy.start()
    row = lax.broadcasted_iota(jnp.int32, (8, LANES), 0)
    lane = lax.broadcasted_iota(jnp.int32, (8, LANES), 1)
    out_ref[pl.ds(STORED, BS), :] = jnp.zeros((BS, BS), out_ref.dtype)
    id_copy.wait()

    def start(n, table):
        place = ids[0, 0, n]
        r, k = place // across, place % across
        read = jnp.where(place < WB * KB, place, n)
        pltpu.make_async_copy(
            panel_ref.at[
                pl.ds(pl.multiple_of(read // across * BS, BS), BS),
                pl.ds(pl.multiple_of(read % across * BS, BS), BS),
            ],
            out_ref.at[pl.ds(pl.multiple_of(n * BS, BS), BS), :],
            sem,
        ).start()
        outer, inner = (r, k) if across == KB else (k, r)
        return jnp.where((row == outer) & (lane == inner), n, table)

    table = lax.fori_loop(0, MAXB, start, jnp.full((8, LANES), MAXB, jnp.int32), unroll=13)
    both = jnp.concatenate([table, table], axis=0).astype(jnp.float32)
    out_ref[pl.ds(TABLE_AT, TABLE), :] = both.astype(out_ref.dtype)
    blocks = out_ref.at[pl.ds(0, STORED), :]
    pltpu.make_async_copy(blocks, blocks, sem).wait()


def gather_blocks(panel, ids, across):
    any_space = pl.BlockSpec(memory_space=pl.ANY)
    return pl.pallas_call(
        functools.partial(gather_blocks_kernel, across),
        out_shape=pltpu.VMEM((PACKED, BS), panel.dtype),
        in_specs=[any_space] * 2,
        out_specs=pl.BlockSpec(memory_space=pltpu.VMEM),
        scratch_shapes=[
            pltpu.SMEM(ids.shape, jnp.int32),
            pltpu.SemaphoreType.DMA,
            pltpu.SemaphoreType.DMA,
        ],
        compiler_params=pltpu.CompilerParams(vmem_limit_bytes=KERNEL_VMEM),
        cost_estimate=pl.CostEstimate(
            flops=0, bytes_accessed=2 * PACKED * BS * 2, transcendentals=0
        ),
    )(
        pltpu.with_memory_space_constraint(ids, pltpu.HBM),
        pltpu.with_memory_space_constraint(panel, pltpu.HBM),
    )


def slot_words(left, right):
    both = (jnp.minimum(left[0:1], left[1:2]) < MAXB) & (jnp.minimum(right[0:1], right[1:2]) < MAXB)
    slots = (left[0:1], left[1:2], right[0:1], right[1:2])
    word = sum(slot << (8 * n) for n, slot in enumerate(slots))
    return jnp.where(both, word, -1)


def multiply(left_ref, right_ref, words, chosen, out_ref):
    def choose(k, count):
        word = words[k]
        chosen[count] = word
        return count + (word >= 0).astype(jnp.int32)

    count = lax.fori_loop(0, KB, choose, 0, unroll=14)
    nothing = MAXB * 0x01010101
    for q in range(GROUP - 1):
        chosen[count + q] = nothing
    out_ref[...] = jnp.zeros(out_ref.shape, out_ref.dtype)

    def block(ref, word, n):
        slot = lax.shift_right_logical(word, 8 * n) & 0xFF
        return ref[pl.ds(pl.multiple_of(slot * BS, BS), BS), :]

    def step(t, carry):
        words = [chosen[t * GROUP + q] for q in range(GROUP)]
        left = jnp.concatenate(
            [
                jnp.concatenate([block(left_ref, word, r) for word in words], axis=1)
                for r in range(WB)
            ],
            axis=0,
        )
        right = jnp.concatenate(
            [
                jnp.concatenate([block(right_ref, word, WB + c) for word in words], axis=0)
                for c in range(WB)
            ],
            axis=1,
        )
        out_ref[...] += jnp.dot(left, right, preferred_element_type=jnp.float32)
        return carry

    lax.fori_loop(0, (count + GROUP - 1) // GROUP, step, 0)


def table_in(ref):
    return ref[pl.ds(TABLE_AT, TABLE), :].astype(jnp.float32).astype(jnp.int32)


def to_scalars(rows, held, words, sem):
    rows = rows + [rows[0]] * (8 - len(rows))
    held[...] = jnp.concatenate(rows, axis=0)
    copy = pltpu.make_async_copy(held, words, sem)
    copy.start()
    copy.wait()


def masked(filter_ref, step, value):
    rows = []
    for r in range(WB):
        row = []
        for c in range(WB):
            block = value[r * BS : (r + 1) * BS, c * BS : (c + 1) * BS]
            row.append(jnp.where(filter_ref[step, r, c] == 1, block, 0.0))
        rows.append(jnp.concatenate(row, axis=1))
    return jnp.concatenate(rows, axis=0)


def base_kernel(filter_ref, own_ref, one_ref, before_ref, out_ref):
    odd = lax.axis_index("row") % 2
    one = masked(filter_ref, 3 - 2 * odd, one_ref[...].astype(jnp.float32))
    total = masked(filter_ref, 0, own_ref[...]) + one
    out_ref[...] = 2.0 * total - before_ref[...].astype(jnp.float32)


def send_product(left_ref, right_ref, words, chosen, product, out_ref):
    multiply(left_ref, right_ref, words, chosen, product)
    out_ref[...] = product[...].astype(out_ref.dtype)


def own_kernel(left_near_ref, left_ref, right_ref, own_ref, held, words, chosen, sem):
    to_scalars([slot_words(table_in(left_ref), table_in(right_ref))], held, words, sem)
    multiply(left_ref, right_ref, words.at[0], chosen, own_ref)


def early_kernel(
    own_ref,
    left_near_ref,
    right_far_ref,
    right_own_ref,
    one_ref,
    product,
    held,
    words,
    chosen,
    sem,
):
    odd = lax.axis_index("row") % 2 == 1
    right_other = jnp.where(odd, table_in(right_far_ref), table_in(right_own_ref))
    to_scalars([slot_words(table_in(left_near_ref), right_other)], held, words, sem)

    @pl.when(odd)
    def _():
        send_product(left_near_ref, right_far_ref, words.at[0], chosen, product, one_ref)

    @pl.when(jnp.logical_not(odd))
    def _():
        send_product(left_near_ref, right_own_ref, words.at[0], chosen, product, one_ref)


def late_kernel(
    one_ref,
    left_near_ref,
    right_near_ref,
    left_far_ref,
    left_own_ref,
    two_ref,
    three_ref,
    product,
    held,
    words,
    chosen,
    sem,
):
    odd = lax.axis_index("row") % 2 == 1
    right_near = table_in(right_near_ref)
    left_other = jnp.where(odd, table_in(left_far_ref), table_in(left_own_ref))
    to_scalars(
        [slot_words(table_in(left_near_ref), right_near), slot_words(left_other, right_near)],
        held,
        words,
        sem,
    )
    send_product(left_near_ref, right_near_ref, words.at[0], chosen, product, two_ref)

    @pl.when(odd)
    def _():
        send_product(left_far_ref, right_near_ref, words.at[1], chosen, product, three_ref)

    @pl.when(jnp.logical_not(odd))
    def _():
        send_product(left_own_ref, right_near_ref, words.at[1], chosen, product, three_ref)


def final_kernel(
    filter_ref, coefficient_ref, base_ref, two_ref, three_ref, density_ref, term_out, density_out
):
    odd = lax.axis_index("row") % 2
    two = masked(filter_ref, 2, two_ref[...].astype(jnp.float32))
    three = masked(filter_ref, 1 + 2 * odd, three_ref[...].astype(jnp.float32))
    total = two + three
    term_next = (2.0 * total + base_ref[...]).astype(jnp.bfloat16)
    term_out[...] = term_next
    density_out[...] = density_ref[...] + coefficient_ref[0] * term_next.astype(jnp.float32)


ANYWHERE = pl.BlockSpec(memory_space=pl.ANY)
IN_VMEM = pl.BlockSpec(memory_space=pltpu.VMEM)
IN_SMEM = pl.BlockSpec(memory_space=pltpu.SMEM)
PANEL = (WB * BS, WB * BS)
RESULT = jax.ShapeDtypeStruct(PANEL, jnp.float32)
SENT = jax.ShapeDtypeStruct(PANEL, jnp.bfloat16)
LISTS = [
    pltpu.VMEM((8, LANES), jnp.int32),
    pltpu.SMEM((8, LANES), jnp.int32),
    pltpu.SMEM((LANES,), jnp.int32),
    pltpu.SemaphoreType.DMA,
]


def run_kernel(kernel, in_specs, out_shape, scratch_shapes, products, *args):
    return pl.pallas_call(
        kernel,
        out_shape=out_shape,
        in_specs=in_specs,
        out_specs=[IN_VMEM] * len(out_shape),
        scratch_shapes=scratch_shapes,
        compiler_params=pltpu.CompilerParams(vmem_limit_bytes=KERNEL_VMEM),
        cost_estimate=pl.CostEstimate(
            flops=products * 2 * WB * WB * BS * BS * BS * 40,
            bytes_accessed=4 * len(out_shape) * WB * WB * BS * BS,
            transcendentals=0,
        ),
    )(*args)


def per_device(
    hamiltonian,
    term_now,
    hamiltonian_ids,
    term_ids,
    product_filter,
    term_before,
    density_in,
    coefficient,
):
    left_own = gather_blocks(hamiltonian, hamiltonian_ids, KB)
    left_n = move(left_own, left_near)
    right_own = gather_blocks(term_now, term_ids, WB)
    right_f = move(right_own, right_far)
    right_n = move(right_own, right_near)
    left_f = move(left_own, left_far)

    def in_vmem(panel):
        return pltpu.with_memory_space_constraint(panel, pltpu.VMEM)

    (own,) = run_kernel(
        own_kernel,
        [ANYWHERE] + [IN_VMEM] * 2,
        [RESULT],
        LISTS,
        1,
        left_n,
        in_vmem(left_own),
        in_vmem(right_own),
    )
    (one,) = run_kernel(
        early_kernel,
        [ANYWHERE] + [IN_VMEM] * 3,
        [SENT],
        [pltpu.VMEM(PANEL, jnp.float32)] + LISTS,
        1,
        own,
        *[in_vmem(panel) for panel in (left_n, right_f, right_own)],
    )
    two, three = run_kernel(
        late_kernel,
        [ANYWHERE] + [IN_VMEM] * 4,
        [SENT] * 2,
        [pltpu.VMEM(PANEL, jnp.float32)] + LISTS,
        2,
        one,
        *[in_vmem(panel) for panel in (left_n, right_n, left_f, left_own)],
    )
    two, three, one = move(two, home_two), move(three, home_three), move(one, home_one)
    (base,) = run_kernel(
        base_kernel,
        [IN_SMEM] + [IN_VMEM] * 3,
        [RESULT],
        [],
        0,
        product_filter,
        own,
        one,
        term_before,
    )
    term_next, density_out = run_kernel(
        final_kernel,
        [IN_SMEM] * 2 + [IN_VMEM] * 4,
        [
            jax.ShapeDtypeStruct(term_before.shape, jnp.bfloat16),
            jax.ShapeDtypeStruct(density_in.shape, jnp.float32),
        ],
        [],
        0,
        product_filter,
        coefficient,
        base,
        two,
        three,
        density_in,
    )
    return (term_next, density_out)


def solution(mesh):
    return jax.shard_map(
        per_device,
        mesh=mesh,
        in_specs=(
            P("row", "col"),
            P("row", "col"),
            P("row", "col", None),
            P("row", "col", None),
            P(None, "row", "col"),
            P("row", "col"),
            P("row", "col"),
            P(),
        ),
        out_specs=(P("row", "col"), P("row", "col")),
        check_vma=False,
    )
```

```python
import functools

import jax
import jax.numpy as jnp
from jax import lax
from jax.experimental import pallas as pl
from jax.experimental.pallas import tpu as pltpu
from jax.sharding import PartitionSpec as P

BS = 128
KB = 98
WB = 2
STEPS = 4
MAXB = 78
N_ROW = 8
N_COL = 16
AXES = ("row", "col")
GROUP = 24
LANES = 128
KERNEL_VMEM = 6 * 1024 * 1024
STORED = MAXB * BS
TABLE_AT = STORED + BS
TABLE = 16
PACKED = TABLE_AT + TABLE


def left_near(i, j):
    if i % 2 == 1:
        return i - 1, j + 1
    return i - 1, j - 1 if j % 4 == 1 else j + 3


def right_near(i, j):
    if i % 2 == 1:
        return i + 1, j - 1
    return i + 1, j - 3 if j % 4 == 3 else j + 1


def left_far(i, j):
    if i % 2 == 1:
        return i - 2, j if j % 4 == 0 else j + 4
    return None


def right_far(i, j):
    if i % 2 == 1:
        return i + 2, j - 4 if j % 4 == 0 else j
    return None


def home_two(i, j):
    if i % 2 == 1:
        return i + 1, j + 3 if j % 4 == 0 else j - 1
    return i + 1, j + 1


def home_three(i, j):
    if i % 2 == 1:
        return i + 2, j + 3 if j % 4 == 0 else j - 1
    return i, j + 1


def home_one(i, j):
    if i % 2 == 1:
        return i + 1, j + 4 if j % 4 == 0 else j
    return i + 1, j


def move(value, target):
    pairs = []
    for i in range(N_ROW):
        for j in range(N_COL):
            to = target(i, j)
            if to is not None:
                pairs.append((i * N_COL + j, (to[0] % N_ROW) * N_COL + to[1] % N_COL))
    return lax.ppermute(value, AXES, pairs)


def gather_blocks_kernel(
    left_ids_ref, right_ids_ref, left_ref, right_ref, left_out, right_out, left_ids, right_ids, id_sems, sems
):
    id_copies = [
        pltpu.make_async_copy(source, target, id_sems.at[n])
        for n, (source, target) in enumerate(
            ((left_ids_ref, left_ids), (right_ids_ref, right_ids))
        )
    ]
    for copy in id_copies:
        copy.start()
    row = lax.broadcasted_iota(jnp.int32, (8, LANES), 0)
    lane = lax.broadcasted_iota(jnp.int32, (8, LANES), 1)
    sides = ((left_ids, left_ref, left_out, KB), (right_ids, right_ref, right_out, WB))
    tables = []
    for side, (ids, panel_ref, out_ref, across) in enumerate(sides):
        id_copies[side].wait()

        def start(n, table):
            place = ids[0, 0, n]
            r, k = place // across, place % across
            read = jnp.where(place < WB * KB, place, n)
            pltpu.make_async_copy(
                panel_ref.at[
                    pl.ds(pl.multiple_of(read // across * BS, BS), BS),
                    pl.ds(pl.multiple_of(read % across * BS, BS), BS),
                ],
                out_ref.at[pl.ds(pl.multiple_of(n * BS, BS), BS), :],
                sems.at[side],
            ).start()
            outer, inner = (r, k) if across == KB else (k, r)
            return jnp.where((row == outer) & (lane == inner), n, table)

        tables.append(
            lax.fori_loop(0, MAXB, start, jnp.full((8, LANES), MAXB, jnp.int32), unroll=13)
        )
    for (_, _, out_ref, _), table in zip(sides, tables):
        out_ref[pl.ds(STORED, BS), :] = jnp.zeros((BS, BS), out_ref.dtype)
        both = jnp.concatenate([table, table], axis=0).astype(jnp.float32)
        out_ref[pl.ds(TABLE_AT, TABLE), :] = both.astype(out_ref.dtype)
    for side, (_, _, out_ref, _) in enumerate(sides):
        blocks = out_ref.at[pl.ds(0, STORED), :]
        pltpu.make_async_copy(blocks, blocks, sems.at[side]).wait()


def gather_blocks(left, right, left_ids, right_ids):
    any_space = pl.BlockSpec(memory_space=pl.ANY)
    return pl.pallas_call(
        gather_blocks_kernel,
        out_shape=[pltpu.VMEM((PACKED, BS), left.dtype)] * 2,
        in_specs=[any_space] * 4,
        out_specs=[pl.BlockSpec(memory_space=pltpu.VMEM)] * 2,
        scratch_shapes=[
            pltpu.SMEM(left_ids.shape, jnp.int32),
            pltpu.SMEM(right_ids.shape, jnp.int32),
            pltpu.SemaphoreType.DMA((2,)),
            pltpu.SemaphoreType.DMA((2,)),
        ],
        compiler_params=pltpu.CompilerParams(vmem_limit_bytes=KERNEL_VMEM),
        cost_estimate=pl.CostEstimate(
            flops=0, bytes_accessed=4 * PACKED * BS * 2, transcendentals=0
        ),
    )(
        pltpu.with_memory_space_constraint(left_ids, pltpu.HBM),
        pltpu.with_memory_space_constraint(right_ids, pltpu.HBM),
        pltpu.with_memory_space_constraint(left, pltpu.HBM),
        pltpu.with_memory_space_constraint(right, pltpu.HBM),
    )


def slot_words(left, right):
    both = (jnp.minimum(left[0:1], left[1:2]) < MAXB) & (jnp.minimum(right[0:1], right[1:2]) < MAXB)
    slots = (left[0:1], left[1:2], right[0:1], right[1:2])
    word = sum(slot << (8 * n) for n, slot in enumerate(slots))
    return jnp.where(both, word, -1)


def multiply(left_ref, right_ref, words, chosen, out_ref):
    def choose(k, count):
        word = words[k]
        chosen[count] = word
        return count + (word >= 0).astype(jnp.int32)

    count = lax.fori_loop(0, KB, choose, 0, unroll=14)
    nothing = MAXB * 0x01010101
    for q in range(GROUP - 1):
        chosen[count + q] = nothing
    out_ref[...] = jnp.zeros(out_ref.shape, out_ref.dtype)

    def block(ref, word, n):
        slot = lax.shift_right_logical(word, 8 * n) & 0xFF
        return ref[pl.ds(pl.multiple_of(slot * BS, BS), BS), :]

    def step(t, carry):
        words = [chosen[t * GROUP + q] for q in range(GROUP)]
        left = jnp.concatenate(
            [
                jnp.concatenate([block(left_ref, word, r) for word in words], axis=1)
                for r in range(WB)
            ],
            axis=0,
        )
        right = jnp.concatenate(
            [
                jnp.concatenate([block(right_ref, word, WB + c) for word in words], axis=0)
                for c in range(WB)
            ],
            axis=1,
        )
        out_ref[...] += jnp.dot(left, right, preferred_element_type=jnp.float32)
        return carry

    lax.fori_loop(0, (count + GROUP - 1) // GROUP, step, 0)


def table_in(ref):
    return ref[pl.ds(TABLE_AT, TABLE), :].astype(jnp.float32).astype(jnp.int32)


def to_scalars(rows, held, words, sem):
    rows = rows + [rows[0]] * (8 - len(rows))
    held[...] = jnp.concatenate(rows, axis=0)
    copy = pltpu.make_async_copy(held, words, sem)
    copy.start()
    copy.wait()


def masked(filter_ref, step, value):
    rows = []
    for r in range(WB):
        row = []
        for c in range(WB):
            block = value[r * BS : (r + 1) * BS, c * BS : (c + 1) * BS]
            row.append(jnp.where(filter_ref[step, r, c] == 1, block, 0.0))
        rows.append(jnp.concatenate(row, axis=1))
    return jnp.concatenate(rows, axis=0)


def base_kernel(filter_ref, own_ref, one_ref, before_ref, out_ref):
    odd = lax.axis_index("row") % 2
    one = masked(filter_ref, 3 - 2 * odd, one_ref[...].astype(jnp.float32))
    total = masked(filter_ref, 0, own_ref[...]) + one
    out_ref[...] = 2.0 * total - before_ref[...].astype(jnp.float32)


def send_product(left_ref, right_ref, words, chosen, product, out_ref):
    multiply(left_ref, right_ref, words, chosen, product)
    out_ref[...] = product[...].astype(out_ref.dtype)


def own_kernel(left_ref, right_ref, own_ref, held, words, chosen, sem):
    to_scalars([slot_words(table_in(left_ref), table_in(right_ref))], held, words, sem)
    multiply(left_ref, right_ref, words.at[0], chosen, own_ref)


def early_kernel(
    own_ref,
    left_near_ref,
    right_far_ref,
    right_own_ref,
    one_ref,
    product,
    held,
    words,
    chosen,
    sem,
):
    odd = lax.axis_index("row") % 2 == 1
    right_other = jnp.where(odd, table_in(right_far_ref), table_in(right_own_ref))
    to_scalars([slot_words(table_in(left_near_ref), right_other)], held, words, sem)

    @pl.when(odd)
    def _():
        send_product(left_near_ref, right_far_ref, words.at[0], chosen, product, one_ref)

    @pl.when(jnp.logical_not(odd))
    def _():
        send_product(left_near_ref, right_own_ref, words.at[0], chosen, product, one_ref)


def late_kernel(
    one_ref,
    left_near_ref,
    right_near_ref,
    left_far_ref,
    left_own_ref,
    two_ref,
    three_ref,
    product,
    held,
    words,
    chosen,
    sem,
):
    odd = lax.axis_index("row") % 2 == 1
    right_near = table_in(right_near_ref)
    left_other = jnp.where(odd, table_in(left_far_ref), table_in(left_own_ref))
    to_scalars(
        [slot_words(table_in(left_near_ref), right_near), slot_words(left_other, right_near)],
        held,
        words,
        sem,
    )
    send_product(left_near_ref, right_near_ref, words.at[0], chosen, product, two_ref)

    @pl.when(odd)
    def _():
        send_product(left_far_ref, right_near_ref, words.at[1], chosen, product, three_ref)

    @pl.when(jnp.logical_not(odd))
    def _():
        send_product(left_own_ref, right_near_ref, words.at[1], chosen, product, three_ref)


def final_kernel(
    filter_ref, coefficient_ref, base_ref, two_ref, three_ref, density_ref, term_out, density_out
):
    odd = lax.axis_index("row") % 2
    two = masked(filter_ref, 2, two_ref[...].astype(jnp.float32))
    three = masked(filter_ref, 1 + 2 * odd, three_ref[...].astype(jnp.float32))
    total = two + three
    term_next = (2.0 * total + base_ref[...]).astype(jnp.bfloat16)
    term_out[...] = term_next
    density_out[...] = density_ref[...] + coefficient_ref[0] * term_next.astype(jnp.float32)


ANYWHERE = pl.BlockSpec(memory_space=pl.ANY)
IN_VMEM = pl.BlockSpec(memory_space=pltpu.VMEM)
IN_SMEM = pl.BlockSpec(memory_space=pltpu.SMEM)
PANEL = (WB * BS, WB * BS)
RESULT = jax.ShapeDtypeStruct(PANEL, jnp.float32)
SENT = jax.ShapeDtypeStruct(PANEL, jnp.bfloat16)
LISTS = [
    pltpu.VMEM((8, LANES), jnp.int32),
    pltpu.SMEM((8, LANES), jnp.int32),
    pltpu.SMEM((LANES,), jnp.int32),
    pltpu.SemaphoreType.DMA,
]


def run_kernel(kernel, in_specs, out_shape, scratch_shapes, products, *args):
    return pl.pallas_call(
        kernel,
        out_shape=out_shape,
        in_specs=in_specs,
        out_specs=[IN_VMEM] * len(out_shape),
        scratch_shapes=scratch_shapes,
        compiler_params=pltpu.CompilerParams(vmem_limit_bytes=KERNEL_VMEM),
        cost_estimate=pl.CostEstimate(
            flops=products * 2 * WB * WB * BS * BS * BS * 40,
            bytes_accessed=4 * len(out_shape) * WB * WB * BS * BS,
            transcendentals=0,
        ),
    )(*args)


def per_device(
    hamiltonian,
    term_now,
    hamiltonian_ids,
    term_ids,
    product_filter,
    term_before,
    density_in,
    coefficient,
):
    left_own, right_own = gather_blocks(hamiltonian, term_now, hamiltonian_ids, term_ids)
    left_n = move(left_own, left_near)
    right_f = move(right_own, right_far)
    right_n = move(right_own, right_near)
    left_f = move(left_own, left_far)

    def in_vmem(panel):
        return pltpu.with_memory_space_constraint(panel, pltpu.VMEM)

    (own,) = run_kernel(
        own_kernel,
        [IN_VMEM] * 2,
        [RESULT],
        LISTS,
        1,
        in_vmem(left_own),
        in_vmem(right_own),
    )
    (one,) = run_kernel(
        early_kernel,
        [ANYWHERE] + [IN_VMEM] * 3,
        [SENT],
        [pltpu.VMEM(PANEL, jnp.float32)] + LISTS,
        1,
        own,
        *[in_vmem(panel) for panel in (left_n, right_f, right_own)],
    )
    two, three = run_kernel(
        late_kernel,
        [ANYWHERE] + [IN_VMEM] * 4,
        [SENT] * 2,
        [pltpu.VMEM(PANEL, jnp.float32)] + LISTS,
        2,
        one,
        *[in_vmem(panel) for panel in (left_n, right_n, left_f, left_own)],
    )
    two, three, one = move(two, home_two), move(three, home_three), move(one, home_one)
    (base,) = run_kernel(
        base_kernel,
        [IN_SMEM] + [IN_VMEM] * 3,
        [RESULT],
        [],
        0,
        product_filter,
        own,
        one,
        term_before,
    )
    term_next, density_out = run_kernel(
        final_kernel,
        [IN_SMEM] * 2 + [IN_VMEM] * 4,
        [
            jax.ShapeDtypeStruct(term_before.shape, jnp.bfloat16),
            jax.ShapeDtypeStruct(density_in.shape, jnp.float32),
        ],
        [],
        0,
        product_filter,
        coefficient,
        base,
        two,
        three,
        density_in,
    )
    return (term_next, density_out)


def solution(mesh):
    return jax.shard_map(
        per_device,
        mesh=mesh,
        in_specs=(
            P("row", "col"),
            P("row", "col"),
            P("row", "col", None),
            P("row", "col", None),
            P(None, "row", "col"),
            P("row", "col"),
            P("row", "col"),
            P(),
        ),
        out_specs=(P("row", "col"), P("row", "col")),
        check_vma=False,
    )
```

```python
import functools

import jax
import jax.numpy as jnp
from jax import lax
from jax.experimental import pallas as pl
from jax.experimental.pallas import tpu as pltpu
from jax.sharding import PartitionSpec as P

BS = 128
KB = 98
WB = 2
STEPS = 4
MAXB = 78
N_ROW = 8
N_COL = 16
AXES = ("row", "col")
GROUP = 24
LANES = 128
KERNEL_VMEM = 6 * 1024 * 1024
STORED = MAXB * BS
TABLE_AT = STORED + BS
TABLE = 16
PACKED = TABLE_AT + TABLE


def left_near(i, j):
    if i % 2 == 1:
        return i - 1, j + 1
    return i - 1, j - 1 if j % 4 == 1 else j + 3


def right_near(i, j):
    if i % 2 == 1:
        return i + 1, j - 1
    return i + 1, j - 3 if j % 4 == 3 else j + 1


def left_far(i, j):
    if i % 2 == 1:
        return i - 2, j if j % 4 == 0 else j + 4
    return None


def right_far(i, j):
    if i % 2 == 1:
        return i + 2, j - 4 if j % 4 == 0 else j
    return None


def home_two(i, j):
    if i % 2 == 1:
        return i + 1, j + 3 if j % 4 == 0 else j - 1
    return i + 1, j + 1


def home_three(i, j):
    if i % 2 == 1:
        return i + 2, j + 3 if j % 4 == 0 else j - 1
    return i, j + 1


def home_one(i, j):
    if i % 2 == 1:
        return i + 1, j + 4 if j % 4 == 0 else j
    return i + 1, j


def move(value, target):
    pairs = []
    for i in range(N_ROW):
        for j in range(N_COL):
            to = target(i, j)
            if to is not None:
                pairs.append((i * N_COL + j, (to[0] % N_ROW) * N_COL + to[1] % N_COL))
    return lax.ppermute(value, AXES, pairs)


def gather_blocks_kernel(
    left_ids_ref, right_ids_ref, left_ref, right_ref, left_out, right_out, left_ids, right_ids, id_sems, sems
):
    id_copies = [
        pltpu.make_async_copy(source, target, id_sems.at[n])
        for n, (source, target) in enumerate(
            ((left_ids_ref, left_ids), (right_ids_ref, right_ids))
        )
    ]
    for copy in id_copies:
        copy.start()
    row = lax.broadcasted_iota(jnp.int32, (8, LANES), 0)
    lane = lax.broadcasted_iota(jnp.int32, (8, LANES), 1)
    sides = ((left_ids, left_ref, left_out, KB), (right_ids, right_ref, right_out, WB))
    tables = []
    for side, (ids, panel_ref, out_ref, across) in enumerate(sides):
        id_copies[side].wait()

        def start(n, table):
            place = ids[0, 0, n]
            r, k = place // across, place % across
            at = pl.ds(pl.multiple_of(n * BS, BS), BS)

            @pl.when(place < WB * KB)
            def _():
                pltpu.make_async_copy(
                    panel_ref.at[
                        pl.ds(pl.multiple_of(r * BS, BS), BS), pl.ds(pl.multiple_of(k * BS, BS), BS)
                    ],
                    out_ref.at[at, :],
                    sems.at[side],
                ).start()

            outer, inner = (r, k) if across == KB else (k, r)
            return jnp.where((row == outer) & (lane == inner), n, table)

        tables.append(
            lax.fori_loop(0, MAXB, start, jnp.full((8, LANES), MAXB, jnp.int32), unroll=13)
        )
    for (_, _, out_ref, _), table in zip(sides, tables):
        out_ref[pl.ds(STORED, BS), :] = jnp.zeros((BS, BS), out_ref.dtype)
        both = jnp.concatenate([table, table], axis=0).astype(jnp.float32)
        out_ref[pl.ds(TABLE_AT, TABLE), :] = both.astype(out_ref.dtype)
    for side, (ids, _, out_ref, _) in enumerate(sides):

        def finish(n, carry):
            @pl.when(ids[0, 0, n] < WB * KB)
            def _():
                block = out_ref.at[pl.ds(0, BS), :]
                pltpu.make_async_copy(block, block, sems.at[side]).wait()

            return carry

        lax.fori_loop(0, MAXB, finish, 0, unroll=13)


def gather_blocks(left, right, left_ids, right_ids):
    any_space = pl.BlockSpec(memory_space=pl.ANY)
    return pl.pallas_call(
        gather_blocks_kernel,
        out_shape=[pltpu.VMEM((PACKED, BS), left.dtype)] * 2,
        in_specs=[any_space] * 4,
        out_specs=[pl.BlockSpec(memory_space=pltpu.VMEM)] * 2,
        scratch_shapes=[
            pltpu.SMEM(left_ids.shape, jnp.int32),
            pltpu.SMEM(right_ids.shape, jnp.int32),
            pltpu.SemaphoreType.DMA((2,)),
            pltpu.SemaphoreType.DMA((2,)),
        ],
        compiler_params=pltpu.CompilerParams(vmem_limit_bytes=KERNEL_VMEM),
        cost_estimate=pl.CostEstimate(
            flops=0, bytes_accessed=4 * PACKED * BS * 2, transcendentals=0
        ),
    )(
        pltpu.with_memory_space_constraint(left_ids, pltpu.HBM),
        pltpu.with_memory_space_constraint(right_ids, pltpu.HBM),
        pltpu.with_memory_space_constraint(left, pltpu.HBM),
        pltpu.with_memory_space_constraint(right, pltpu.HBM),
    )


def slot_words(left, right):
    both = (jnp.minimum(left[0:1], left[1:2]) < MAXB) & (jnp.minimum(right[0:1], right[1:2]) < MAXB)
    slots = (left[0:1], left[1:2], right[0:1], right[1:2])
    word = sum(slot << (8 * n) for n, slot in enumerate(slots))
    return jnp.where(both, word, -1)


def multiply(left_ref, right_ref, words, chosen, out_ref):
    def choose(k, count):
        word = words[k]
        chosen[count] = word
        return count + (word >= 0).astype(jnp.int32)

    count = lax.fori_loop(0, KB, choose, 0, unroll=14)
    nothing = MAXB * 0x01010101
    for q in range(GROUP - 1):
        chosen[count + q] = nothing
    out_ref[...] = jnp.zeros(out_ref.shape, out_ref.dtype)

    def block(ref, word, n):
        slot = lax.shift_right_logical(word, 8 * n) & 0xFF
        return ref[pl.ds(pl.multiple_of(slot * BS, BS), BS), :]

    def step(t, carry):
        words = [chosen[t * GROUP + q] for q in range(GROUP)]
        left = jnp.concatenate(
            [
                jnp.concatenate([block(left_ref, word, r) for word in words], axis=1)
                for r in range(WB)
            ],
            axis=0,
        )
        right = jnp.concatenate(
            [
                jnp.concatenate([block(right_ref, word, WB + c) for word in words], axis=0)
                for c in range(WB)
            ],
            axis=1,
        )
        out_ref[...] += jnp.dot(left, right, preferred_element_type=jnp.float32)
        return carry

    lax.fori_loop(0, (count + GROUP - 1) // GROUP, step, 0)


def table_in(ref):
    return ref[pl.ds(TABLE_AT, TABLE), :].astype(jnp.float32).astype(jnp.int32)


def to_scalars(rows, held, words, sem):
    rows = rows + [rows[0]] * (8 - len(rows))
    held[...] = jnp.concatenate(rows, axis=0)
    copy = pltpu.make_async_copy(held, words, sem)
    copy.start()
    copy.wait()


def masked(filter_ref, step, value):
    rows = []
    for r in range(WB):
        row = []
        for c in range(WB):
            block = value[r * BS : (r + 1) * BS, c * BS : (c + 1) * BS]
            row.append(jnp.where(filter_ref[step, r, c] == 1, block, 0.0))
        rows.append(jnp.concatenate(row, axis=1))
    return jnp.concatenate(rows, axis=0)


def base_kernel(filter_ref, own_ref, one_ref, before_ref, out_ref):
    odd = lax.axis_index("row") % 2
    one = masked(filter_ref, 3 - 2 * odd, one_ref[...].astype(jnp.float32))
    total = masked(filter_ref, 0, own_ref[...]) + one
    out_ref[...] = 2.0 * total - before_ref[...].astype(jnp.float32)


def send_product(left_ref, right_ref, words, chosen, product, out_ref):
    multiply(left_ref, right_ref, words, chosen, product)
    out_ref[...] = product[...].astype(out_ref.dtype)


def own_kernel(left_ref, right_ref, own_ref, held, words, chosen, sem):
    to_scalars([slot_words(table_in(left_ref), table_in(right_ref))], held, words, sem)
    multiply(left_ref, right_ref, words.at[0], chosen, own_ref)


def early_kernel(
    own_ref,
    left_near_ref,
    right_far_ref,
    right_own_ref,
    one_ref,
    product,
    held,
    words,
    chosen,
    sem,
):
    odd = lax.axis_index("row") % 2 == 1
    right_other = jnp.where(odd, table_in(right_far_ref), table_in(right_own_ref))
    to_scalars([slot_words(table_in(left_near_ref), right_other)], held, words, sem)

    @pl.when(odd)
    def _():
        send_product(left_near_ref, right_far_ref, words.at[0], chosen, product, one_ref)

    @pl.when(jnp.logical_not(odd))
    def _():
        send_product(left_near_ref, right_own_ref, words.at[0], chosen, product, one_ref)


def late_kernel(
    one_ref,
    left_near_ref,
    right_near_ref,
    left_far_ref,
    left_own_ref,
    two_ref,
    three_ref,
    product,
    held,
    words,
    chosen,
    sem,
):
    odd = lax.axis_index("row") % 2 == 1
    right_near = table_in(right_near_ref)
    left_other = jnp.where(odd, table_in(left_far_ref), table_in(left_own_ref))
    to_scalars(
        [slot_words(table_in(left_near_ref), right_near), slot_words(left_other, right_near)],
        held,
        words,
        sem,
    )
    send_product(left_near_ref, right_near_ref, words.at[0], chosen, product, two_ref)

    @pl.when(odd)
    def _():
        send_product(left_far_ref, right_near_ref, words.at[1], chosen, product, three_ref)

    @pl.when(jnp.logical_not(odd))
    def _():
        send_product(left_own_ref, right_near_ref, words.at[1], chosen, product, three_ref)


def final_kernel(
    filter_ref, coefficient_ref, base_ref, two_ref, three_ref, density_ref, term_out, density_out
):
    odd = lax.axis_index("row") % 2
    two = masked(filter_ref, 2, two_ref[...].astype(jnp.float32))
    three = masked(filter_ref, 1 + 2 * odd, three_ref[...].astype(jnp.float32))
    total = two + three
    term_next = (2.0 * total + base_ref[...]).astype(jnp.bfloat16)
    term_out[...] = term_next
    density_out[...] = density_ref[...] + coefficient_ref[0] * term_next.astype(jnp.float32)


ANYWHERE = pl.BlockSpec(memory_space=pl.ANY)
IN_VMEM = pl.BlockSpec(memory_space=pltpu.VMEM)
IN_SMEM = pl.BlockSpec(memory_space=pltpu.SMEM)
PANEL = (WB * BS, WB * BS)
RESULT = jax.ShapeDtypeStruct(PANEL, jnp.float32)
SENT = jax.ShapeDtypeStruct(PANEL, jnp.bfloat16)
LISTS = [
    pltpu.VMEM((8, LANES), jnp.int32),
    pltpu.SMEM((8, LANES), jnp.int32),
    pltpu.SMEM((LANES,), jnp.int32),
    pltpu.SemaphoreType.DMA,
]


def run_kernel(kernel, in_specs, out_shape, scratch_shapes, products, *args):
    return pl.pallas_call(
        kernel,
        out_shape=out_shape,
        in_specs=in_specs,
        out_specs=[IN_VMEM] * len(out_shape),
        scratch_shapes=scratch_shapes,
        compiler_params=pltpu.CompilerParams(vmem_limit_bytes=KERNEL_VMEM),
        cost_estimate=pl.CostEstimate(
            flops=products * 2 * WB * WB * BS * BS * BS * 40,
            bytes_accessed=4 * len(out_shape) * WB * WB * BS * BS,
            transcendentals=0,
        ),
    )(*args)


def per_device(
    hamiltonian,
    term_now,
    hamiltonian_ids,
    term_ids,
    product_filter,
    term_before,
    density_in,
    coefficient,
):
    left_own, right_own = gather_blocks(hamiltonian, term_now, hamiltonian_ids, term_ids)
    left_n = move(left_own, left_near)
    right_f = move(right_own, right_far)
    right_n = move(right_own, right_near)
    left_f = move(left_own, left_far)

    def in_vmem(panel):
        return pltpu.with_memory_space_constraint(panel, pltpu.VMEM)

    (own,) = run_kernel(
        own_kernel,
        [IN_VMEM] * 2,
        [RESULT],
        LISTS,
        1,
        in_vmem(left_own),
        in_vmem(right_own),
    )
    (one,) = run_kernel(
        early_kernel,
        [ANYWHERE] + [IN_VMEM] * 3,
        [SENT],
        [pltpu.VMEM(PANEL, jnp.float32)] + LISTS,
        1,
        own,
        *[in_vmem(panel) for panel in (left_n, right_f, right_own)],
    )
    two, three = run_kernel(
        late_kernel,
        [ANYWHERE] + [IN_VMEM] * 4,
        [SENT] * 2,
        [pltpu.VMEM(PANEL, jnp.float32)] + LISTS,
        2,
        one,
        *[in_vmem(panel) for panel in (left_n, right_n, left_f, left_own)],
    )
    two, three, one = move(two, home_two), move(three, home_three), move(one, home_one)
    (base,) = run_kernel(
        base_kernel,
        [IN_SMEM] + [IN_VMEM] * 3,
        [RESULT],
        [],
        0,
        product_filter,
        own,
        one,
        term_before,
    )
    term_next, density_out = run_kernel(
        final_kernel,
        [IN_SMEM] * 2 + [IN_VMEM] * 4,
        [
            jax.ShapeDtypeStruct(term_before.shape, jnp.bfloat16),
            jax.ShapeDtypeStruct(density_in.shape, jnp.float32),
        ],
        [],
        0,
        product_filter,
        coefficient,
        base,
        two,
        three,
        density_in,
    )
    return (term_next, density_out)


def solution(mesh):
    return jax.shard_map(
        per_device,
        mesh=mesh,
        in_specs=(
            P("row", "col"),
            P("row", "col"),
            P("row", "col", None),
            P("row", "col", None),
            P(None, "row", "col"),
            P("row", "col"),
            P("row", "col"),
            P(),
        ),
        out_specs=(P("row", "col"), P("row", "col")),
        check_vma=False,
    )
```

```python
import functools

import jax
import jax.numpy as jnp
from jax import lax
from jax.experimental import pallas as pl
from jax.experimental.pallas import tpu as pltpu
from jax.sharding import PartitionSpec as P

BS = 128
KB = 98
WB = 2
STEPS = 4
MAXB = 78
N_ROW = 8
N_COL = 16
AXES = ("row", "col")
GROUP = 24
LANES = 128
KERNEL_VMEM = 6 * 1024 * 1024
STORED = MAXB * BS
TABLE_AT = STORED + BS
TABLE = 16
PACKED = TABLE_AT + TABLE


def left_near(i, j):
    if i % 2 == 1:
        return i - 1, j + 1
    return i - 1, j - 1 if j % 4 == 1 else j + 3


def right_near(i, j):
    if i % 2 == 1:
        return i + 1, j - 1
    return i + 1, j - 3 if j % 4 == 3 else j + 1


def left_far(i, j):
    if i % 2 == 1:
        return i - 2, j if j % 4 == 0 else j + 4
    return None


def right_far(i, j):
    if i % 2 == 1:
        return i + 2, j - 4 if j % 4 == 0 else j
    return None


def home_two(i, j):
    if i % 2 == 1:
        return i + 1, j + 3 if j % 4 == 0 else j - 1
    return i + 1, j + 1


def home_three(i, j):
    if i % 2 == 1:
        return i + 2, j + 3 if j % 4 == 0 else j - 1
    return i, j + 1


def home_one(i, j):
    if i % 2 == 1:
        return i + 1, j + 4 if j % 4 == 0 else j
    return i + 1, j


def move(value, target):
    pairs = []
    for i in range(N_ROW):
        for j in range(N_COL):
            to = target(i, j)
            if to is not None:
                pairs.append((i * N_COL + j, (to[0] % N_ROW) * N_COL + to[1] % N_COL))
    return lax.ppermute(value, AXES, pairs)


def gather_blocks_kernel(
    left_ids_ref, right_ids_ref, left_ref, right_ref, left_out, right_out, left_ids, right_ids, id_sems, sems
):
    id_copies = [
        pltpu.make_async_copy(source, target, id_sems.at[n])
        for n, (source, target) in enumerate(
            ((left_ids_ref, left_ids), (right_ids_ref, right_ids))
        )
    ]
    for copy in id_copies:
        copy.start()
    row = lax.broadcasted_iota(jnp.int32, (8, LANES), 0)
    lane = lax.broadcasted_iota(jnp.int32, (8, LANES), 1)
    sides = ((left_ids, left_ref, left_out, KB), (right_ids, right_ref, right_out, WB))
    tables = []
    for side, (ids, panel_ref, out_ref, across) in enumerate(sides):
        id_copies[side].wait()

        def start(n, table):
            place = ids[0, 0, n]
            r, k = place // across, place % across
            at = pl.ds(pl.multiple_of(n * BS, BS), BS)

            @pl.when(place < WB * KB)
            def _():
                pltpu.make_async_copy(
                    panel_ref.at[
                        pl.ds(pl.multiple_of(r * BS, BS), BS), pl.ds(pl.multiple_of(k * BS, BS), BS)
                    ],
                    out_ref.at[at, :],
                    sems.at[side],
                ).start()

            outer, inner = (r, k) if across == KB else (k, r)
            return jnp.where((row == outer) & (lane == inner), n, table)

        tables.append(
            lax.fori_loop(0, MAXB, start, jnp.full((8, LANES), MAXB, jnp.int32), unroll=13)
        )
    for (_, _, out_ref, _), table in zip(sides, tables):
        out_ref[pl.ds(STORED, BS), :] = jnp.zeros((BS, BS), out_ref.dtype)
        both = jnp.concatenate([table, table], axis=0).astype(jnp.float32)
        out_ref[pl.ds(TABLE_AT, TABLE), :] = both.astype(out_ref.dtype)
    for side, (ids, _, out_ref, _) in enumerate(sides):

        def finish(n, carry):
            @pl.when(ids[0, 0, n] < WB * KB)
            def _():
                block = out_ref.at[pl.ds(0, BS), :]
                pltpu.make_async_copy(block, block, sems.at[side]).wait()

            return carry

        lax.fori_loop(0, MAXB, finish, 0, unroll=13)


def gather_blocks(left, right, left_ids, right_ids):
    any_space = pl.BlockSpec(memory_space=pl.ANY)
    return pl.pallas_call(
        gather_blocks_kernel,
        out_shape=[pltpu.VMEM((PACKED, BS), left.dtype)] * 2,
        in_specs=[any_space] * 4,
        out_specs=[pl.BlockSpec(memory_space=pltpu.VMEM)] * 2,
        scratch_shapes=[
            pltpu.SMEM(left_ids.shape, jnp.int32),
            pltpu.SMEM(right_ids.shape, jnp.int32),
            pltpu.SemaphoreType.DMA((2,)),
            pltpu.SemaphoreType.DMA((2,)),
        ],
        compiler_params=pltpu.CompilerParams(vmem_limit_bytes=KERNEL_VMEM),
        cost_estimate=pl.CostEstimate(
            flops=0, bytes_accessed=4 * PACKED * BS * 2, transcendentals=0
        ),
    )(
        pltpu.with_memory_space_constraint(left_ids, pltpu.HBM),
        pltpu.with_memory_space_constraint(right_ids, pltpu.HBM),
        pltpu.with_memory_space_constraint(left, pltpu.HBM),
        pltpu.with_memory_space_constraint(right, pltpu.HBM),
    )


def slot_words(left, right):
    both = (jnp.minimum(left[0:1], left[1:2]) < MAXB) & (jnp.minimum(right[0:1], right[1:2]) < MAXB)
    slots = (left[0:1], left[1:2], right[0:1], right[1:2])
    word = sum(slot << (8 * n) for n, slot in enumerate(slots))
    return jnp.where(both, word, -1)


def multiply(left_ref, right_ref, words, chosen, out_ref):
    def choose(k, count):
        word = words[k]
        chosen[count] = word
        return count + (word >= 0).astype(jnp.int32)

    count = lax.fori_loop(0, KB, choose, 0, unroll=14)
    nothing = MAXB * 0x01010101
    for q in range(GROUP - 1):
        chosen[count + q] = nothing
    out_ref[...] = jnp.zeros(out_ref.shape, out_ref.dtype)

    def block(ref, word, n):
        slot = lax.shift_right_logical(word, 8 * n) & 0xFF
        return ref[pl.ds(pl.multiple_of(slot * BS, BS), BS), :]

    def step(t, carry):
        words = [chosen[t * GROUP + q] for q in range(GROUP)]
        left = jnp.concatenate(
            [
                jnp.concatenate([block(left_ref, word, r) for word in words], axis=1)
                for r in range(WB)
            ],
            axis=0,
        )
        right = jnp.concatenate(
            [
                jnp.concatenate([block(right_ref, word, WB + c) for word in words], axis=0)
                for c in range(WB)
            ],
            axis=1,
        )
        out_ref[...] += jnp.dot(left, right, preferred_element_type=jnp.float32)
        return carry

    lax.fori_loop(0, (count + GROUP - 1) // GROUP, step, 0)


def table_in(ref):
    return ref[pl.ds(TABLE_AT, TABLE), :].astype(jnp.float32).astype(jnp.int32)


def to_scalars(rows, held, words, sem):
    rows = rows + [rows[0]] * (8 - len(rows))
    held[...] = jnp.concatenate(rows, axis=0)
    copy = pltpu.make_async_copy(held, words, sem)
    copy.start()
    copy.wait()


def masked(filter_ref, step, value):
    rows = []
    for r in range(WB):
        row = []
        for c in range(WB):
            block = value[r * BS : (r + 1) * BS, c * BS : (c + 1) * BS]
            row.append(jnp.where(filter_ref[step, r, c] == 1, block, 0.0))
        rows.append(jnp.concatenate(row, axis=1))
    return jnp.concatenate(rows, axis=0)


def base_kernel(
    filter_ref, coefficient_ref, own_ref, one_ref, before_ref, out_ref, two_factor, three_factor, scale
):
    odd = lax.axis_index("row") % 2
    one = masked(filter_ref, 3 - 2 * odd, one_ref[...].astype(jnp.float32))
    total = masked(filter_ref, 0, own_ref[...]) + one
    out_ref[...] = 2.0 * total - before_ref[...].astype(jnp.float32)
    twos = jnp.full(PANEL, 2.0, jnp.float32)
    two_factor[...] = masked(filter_ref, 2, twos)
    three_factor[...] = masked(filter_ref, 1 + 2 * odd, twos)
    scale[...] = jnp.full(scale.shape, coefficient_ref[0], jnp.float32)


def send_product(left_ref, right_ref, words, chosen, product, out_ref):
    multiply(left_ref, right_ref, words, chosen, product)
    out_ref[...] = product[...].astype(out_ref.dtype)


def own_kernel(left_ref, right_ref, own_ref, held, words, chosen, sem):
    to_scalars([slot_words(table_in(left_ref), table_in(right_ref))], held, words, sem)
    multiply(left_ref, right_ref, words.at[0], chosen, own_ref)


def early_kernel(
    own_ref,
    left_near_ref,
    right_far_ref,
    right_own_ref,
    one_ref,
    product,
    held,
    words,
    chosen,
    sem,
):
    odd = lax.axis_index("row") % 2 == 1
    right_other = jnp.where(odd, table_in(right_far_ref), table_in(right_own_ref))
    to_scalars([slot_words(table_in(left_near_ref), right_other)], held, words, sem)

    @pl.when(odd)
    def _():
        send_product(left_near_ref, right_far_ref, words.at[0], chosen, product, one_ref)

    @pl.when(jnp.logical_not(odd))
    def _():
        send_product(left_near_ref, right_own_ref, words.at[0], chosen, product, one_ref)


def late_kernel(
    one_ref,
    left_near_ref,
    right_near_ref,
    left_far_ref,
    left_own_ref,
    two_ref,
    three_ref,
    product,
    held,
    words,
    chosen,
    sem,
):
    odd = lax.axis_index("row") % 2 == 1
    right_near = table_in(right_near_ref)
    left_other = jnp.where(odd, table_in(left_far_ref), table_in(left_own_ref))
    to_scalars(
        [slot_words(table_in(left_near_ref), right_near), slot_words(left_other, right_near)],
        held,
        words,
        sem,
    )
    send_product(left_near_ref, right_near_ref, words.at[0], chosen, product, two_ref)

    @pl.when(odd)
    def _():
        send_product(left_far_ref, right_near_ref, words.at[1], chosen, product, three_ref)

    @pl.when(jnp.logical_not(odd))
    def _():
        send_product(left_own_ref, right_near_ref, words.at[1], chosen, product, three_ref)


def final_kernel(
    base_ref, two_factor, three_factor, scale, two_ref, three_ref, density_ref, term_out, density_out
):
    two = two_factor[...] * two_ref[...].astype(jnp.float32)
    three = three_factor[...] * three_ref[...].astype(jnp.float32)
    term_next = (base_ref[...] + (two + three)).astype(jnp.bfloat16)
    term_out[...] = term_next
    density_out[...] = density_ref[...] + scale[0:1, 0:1] * term_next.astype(jnp.float32)


ANYWHERE = pl.BlockSpec(memory_space=pl.ANY)
IN_VMEM = pl.BlockSpec(memory_space=pltpu.VMEM)
IN_SMEM = pl.BlockSpec(memory_space=pltpu.SMEM)
PANEL = (WB * BS, WB * BS)
RESULT = jax.ShapeDtypeStruct(PANEL, jnp.float32)
SENT = jax.ShapeDtypeStruct(PANEL, jnp.bfloat16)
LISTS = [
    pltpu.VMEM((8, LANES), jnp.int32),
    pltpu.SMEM((8, LANES), jnp.int32),
    pltpu.SMEM((LANES,), jnp.int32),
    pltpu.SemaphoreType.DMA,
]


def run_kernel(kernel, in_specs, out_shape, scratch_shapes, products, *args):
    return pl.pallas_call(
        kernel,
        out_shape=out_shape,
        in_specs=in_specs,
        out_specs=[IN_VMEM] * len(out_shape),
        scratch_shapes=scratch_shapes,
        compiler_params=pltpu.CompilerParams(vmem_limit_bytes=KERNEL_VMEM),
        cost_estimate=pl.CostEstimate(
            flops=products * 2 * WB * WB * BS * BS * BS * 40,
            bytes_accessed=4 * len(out_shape) * WB * WB * BS * BS,
            transcendentals=0,
        ),
    )(*args)


def per_device(
    hamiltonian,
    term_now,
    hamiltonian_ids,
    term_ids,
    product_filter,
    term_before,
    density_in,
    coefficient,
):
    left_own, right_own = gather_blocks(hamiltonian, term_now, hamiltonian_ids, term_ids)
    left_n = move(left_own, left_near)
    right_f = move(right_own, right_far)
    right_n = move(right_own, right_near)
    left_f = move(left_own, left_far)

    def in_vmem(panel):
        return pltpu.with_memory_space_constraint(panel, pltpu.VMEM)

    (own,) = run_kernel(
        own_kernel,
        [IN_VMEM] * 2,
        [RESULT],
        LISTS,
        1,
        in_vmem(left_own),
        in_vmem(right_own),
    )
    (one,) = run_kernel(
        early_kernel,
        [ANYWHERE] + [IN_VMEM] * 3,
        [SENT],
        [pltpu.VMEM(PANEL, jnp.float32)] + LISTS,
        1,
        own,
        *[in_vmem(panel) for panel in (left_n, right_f, right_own)],
    )
    two, three = run_kernel(
        late_kernel,
        [ANYWHERE] + [IN_VMEM] * 4,
        [SENT] * 2,
        [pltpu.VMEM(PANEL, jnp.float32)] + LISTS,
        2,
        one,
        *[in_vmem(panel) for panel in (left_n, right_n, left_f, left_own)],
    )
    two, three, one = move(two, home_two), move(three, home_three), move(one, home_one)
    base, two_factor, three_factor, scale = run_kernel(
        base_kernel,
        [IN_SMEM] * 2 + [IN_VMEM] * 3,
        [RESULT] * 3 + [jax.ShapeDtypeStruct((8, LANES), jnp.float32)],
        [],
        0,
        product_filter,
        coefficient,
        own,
        one,
        term_before,
    )
    term_next, density_out = run_kernel(
        final_kernel,
        [IN_VMEM] * 7,
        [
            jax.ShapeDtypeStruct(term_before.shape, jnp.bfloat16),
            jax.ShapeDtypeStruct(density_in.shape, jnp.float32),
        ],
        [],
        0,
        base,
        two_factor,
        three_factor,
        scale,
        two,
        three,
        density_in,
    )
    return (term_next, density_out)


def solution(mesh):
    return jax.shard_map(
        per_device,
        mesh=mesh,
        in_specs=(
            P("row", "col"),
            P("row", "col"),
            P("row", "col", None),
            P("row", "col", None),
            P(None, "row", "col"),
            P("row", "col"),
            P("row", "col"),
            P(),
        ),
        out_specs=(P("row", "col"), P("row", "col")),
        check_vma=False,
    )
```

```python
import functools

import jax
import jax.numpy as jnp
from jax import lax
from jax.experimental import pallas as pl
from jax.experimental.pallas import tpu as pltpu
from jax.sharding import PartitionSpec as P

BS = 128
KB = 98
WB = 2
STEPS = 4
MAXB = 78
N_ROW = 8
N_COL = 16
AXES = ("row", "col")
GROUP = 20
LANES = 128
KERNEL_VMEM = 6 * 1024 * 1024
STORED = MAXB * BS
TABLE_AT = STORED + BS
TABLE = 16
PACKED = TABLE_AT + TABLE


def left_near(i, j):
    if i % 2 == 1:
        return i - 1, j + 1
    return i - 1, j - 1 if j % 4 == 1 else j + 3


def right_near(i, j):
    if i % 2 == 1:
        return i + 1, j - 1
    return i + 1, j - 3 if j % 4 == 3 else j + 1


def left_far(i, j):
    if i % 2 == 1:
        return i - 2, j if j % 4 == 0 else j + 4
    return None


def right_far(i, j):
    if i % 2 == 1:
        return i + 2, j - 4 if j % 4 == 0 else j
    return None


def home_two(i, j):
    if i % 2 == 1:
        return i + 1, j + 3 if j % 4 == 0 else j - 1
    return i + 1, j + 1


def home_three(i, j):
    if i % 2 == 1:
        return i + 2, j + 3 if j % 4 == 0 else j - 1
    return i, j + 1


def home_one(i, j):
    if i % 2 == 1:
        return i + 1, j + 4 if j % 4 == 0 else j
    return i + 1, j


def move(value, target):
    pairs = []
    for i in range(N_ROW):
        for j in range(N_COL):
            to = target(i, j)
            if to is not None:
                pairs.append((i * N_COL + j, (to[0] % N_ROW) * N_COL + to[1] % N_COL))
    return lax.ppermute(value, AXES, pairs)


def gather_blocks_kernel(
    left_ids_ref, right_ids_ref, left_ref, right_ref, left_out, right_out, left_ids, right_ids, id_sems, sems
):
    id_copies = [
        pltpu.make_async_copy(source, target, id_sems.at[n])
        for n, (source, target) in enumerate(
            ((left_ids_ref, left_ids), (right_ids_ref, right_ids))
        )
    ]
    for copy in id_copies:
        copy.start()
    row = lax.broadcasted_iota(jnp.int32, (8, LANES), 0)
    lane = lax.broadcasted_iota(jnp.int32, (8, LANES), 1)
    sides = ((left_ids, left_ref, left_out, KB), (right_ids, right_ref, right_out, WB))
    tables = []
    for side, (ids, panel_ref, out_ref, across) in enumerate(sides):
        id_copies[side].wait()

        def start(n, table):
            place = ids[0, 0, n]
            r, k = place // across, place % across
            at = pl.ds(pl.multiple_of(n * BS, BS), BS)

            @pl.when(place < WB * KB)
            def _():
                pltpu.make_async_copy(
                    panel_ref.at[
                        pl.ds(pl.multiple_of(r * BS, BS), BS), pl.ds(pl.multiple_of(k * BS, BS), BS)
                    ],
                    out_ref.at[at, :],
                    sems.at[side],
                ).start()

            outer, inner = (r, k) if across == KB else (k, r)
            return jnp.where((row == outer) & (lane == inner), n, table)

        tables.append(
            lax.fori_loop(0, MAXB, start, jnp.full((8, LANES), MAXB, jnp.int32), unroll=13)
        )
    for (_, _, out_ref, _), table in zip(sides, tables):
        out_ref[pl.ds(STORED, BS), :] = jnp.zeros((BS, BS), out_ref.dtype)
        both = jnp.concatenate([table, table], axis=0).astype(jnp.float32)
        out_ref[pl.ds(TABLE_AT, TABLE), :] = both.astype(out_ref.dtype)
    for side, (ids, _, out_ref, _) in enumerate(sides):

        def finish(n, carry):
            @pl.when(ids[0, 0, n] < WB * KB)
            def _():
                block = out_ref.at[pl.ds(0, BS), :]
                pltpu.make_async_copy(block, block, sems.at[side]).wait()

            return carry

        lax.fori_loop(0, MAXB, finish, 0, unroll=13)


def gather_blocks(left, right, left_ids, right_ids):
    any_space = pl.BlockSpec(memory_space=pl.ANY)
    return pl.pallas_call(
        gather_blocks_kernel,
        out_shape=[pltpu.VMEM((PACKED, BS), left.dtype)] * 2,
        in_specs=[any_space] * 4,
        out_specs=[pl.BlockSpec(memory_space=pltpu.VMEM)] * 2,
        scratch_shapes=[
            pltpu.SMEM(left_ids.shape, jnp.int32),
            pltpu.SMEM(right_ids.shape, jnp.int32),
            pltpu.SemaphoreType.DMA((2,)),
            pltpu.SemaphoreType.DMA((2,)),
        ],
        compiler_params=pltpu.CompilerParams(vmem_limit_bytes=KERNEL_VMEM),
        cost_estimate=pl.CostEstimate(
            flops=0, bytes_accessed=4 * PACKED * BS * 2, transcendentals=0
        ),
    )(
        pltpu.with_memory_space_constraint(left_ids, pltpu.HBM),
        pltpu.with_memory_space_constraint(right_ids, pltpu.HBM),
        pltpu.with_memory_space_constraint(left, pltpu.HBM),
        pltpu.with_memory_space_constraint(right, pltpu.HBM),
    )


def slot_words(left, right):
    both = (jnp.minimum(left[0:1], left[1:2]) < MAXB) & (jnp.minimum(right[0:1], right[1:2]) < MAXB)
    slots = (left[0:1], left[1:2], right[0:1], right[1:2])
    word = sum(slot << (8 * n) for n, slot in enumerate(slots))
    return jnp.where(both, word, -1)


def multiply(left_ref, right_ref, words, chosen, out_ref):
    def choose(k, count):
        word = words[k]
        chosen[count] = word
        return count + (word >= 0).astype(jnp.int32)

    count = lax.fori_loop(0, KB, choose, 0, unroll=14)
    nothing = MAXB * 0x01010101
    for q in range(GROUP - 1):
        chosen[count + q] = nothing
    out_ref[...] = jnp.zeros(out_ref.shape, out_ref.dtype)

    def block(ref, word, n):
        slot = lax.shift_right_logical(word, 8 * n) & 0xFF
        return ref[pl.ds(pl.multiple_of(slot * BS, BS), BS), :]

    def step(t, carry):
        words = [chosen[t * GROUP + q] for q in range(GROUP)]
        left = jnp.concatenate(
            [
                jnp.concatenate([block(left_ref, word, r) for word in words], axis=1)
                for r in range(WB)
            ],
            axis=0,
        )
        right = jnp.concatenate(
            [
                jnp.concatenate([block(right_ref, word, WB + c) for word in words], axis=0)
                for c in range(WB)
            ],
            axis=1,
        )
        out_ref[...] += jnp.dot(left, right, preferred_element_type=jnp.float32)
        return carry

    lax.fori_loop(0, (count + GROUP - 1) // GROUP, step, 0)


def table_in(ref):
    return ref[pl.ds(TABLE_AT, TABLE), :].astype(jnp.float32).astype(jnp.int32)


def to_scalars(rows, held, words, sem):
    rows = rows + [rows[0]] * (8 - len(rows))
    held[...] = jnp.concatenate(rows, axis=0)
    copy = pltpu.make_async_copy(held, words, sem)
    copy.start()
    copy.wait()


def masked(filter_ref, step, value):
    rows = []
    for r in range(WB):
        row = []
        for c in range(WB):
            block = value[r * BS : (r + 1) * BS, c * BS : (c + 1) * BS]
            row.append(jnp.where(filter_ref[step, r, c] == 1, block, 0.0))
        rows.append(jnp.concatenate(row, axis=1))
    return jnp.concatenate(rows, axis=0)


def base_kernel(
    filter_ref, coefficient_ref, own_ref, one_ref, before_ref, out_ref, two_factor, three_factor, scale
):
    odd = lax.axis_index("row") % 2
    one = masked(filter_ref, 3 - 2 * odd, one_ref[...].astype(jnp.float32))
    total = masked(filter_ref, 0, own_ref[...]) + one
    out_ref[...] = 2.0 * total - before_ref[...].astype(jnp.float32)
    twos = jnp.full(PANEL, 2.0, jnp.float32)
    two_factor[...] = masked(filter_ref, 2, twos)
    three_factor[...] = masked(filter_ref, 1 + 2 * odd, twos)
    scale[...] = jnp.full(scale.shape, coefficient_ref[0], jnp.float32)


def send_product(left_ref, right_ref, words, chosen, product, out_ref):
    multiply(left_ref, right_ref, words, chosen, product)
    out_ref[...] = product[...].astype(out_ref.dtype)


def own_kernel(left_ref, right_ref, own_ref, held, words, chosen, sem):
    to_scalars([slot_words(table_in(left_ref), table_in(right_ref))], held, words, sem)
    multiply(left_ref, right_ref, words.at[0], chosen, own_ref)


def early_kernel(
    own_ref,
    left_near_ref,
    right_far_ref,
    right_own_ref,
    one_ref,
    product,
    held,
    words,
    chosen,
    sem,
):
    odd = lax.axis_index("row") % 2 == 1
    right_other = jnp.where(odd, table_in(right_far_ref), table_in(right_own_ref))
    to_scalars([slot_words(table_in(left_near_ref), right_other)], held, words, sem)

    @pl.when(odd)
    def _():
        send_product(left_near_ref, right_far_ref, words.at[0], chosen, product, one_ref)

    @pl.when(jnp.logical_not(odd))
    def _():
        send_product(left_near_ref, right_own_ref, words.at[0], chosen, product, one_ref)


def late_kernel(
    one_ref,
    left_near_ref,
    right_near_ref,
    left_far_ref,
    left_own_ref,
    two_ref,
    three_ref,
    product,
    held,
    words,
    chosen,
    sem,
):
    odd = lax.axis_index("row") % 2 == 1
    right_near = table_in(right_near_ref)
    left_other = jnp.where(odd, table_in(left_far_ref), table_in(left_own_ref))
    to_scalars(
        [slot_words(table_in(left_near_ref), right_near), slot_words(left_other, right_near)],
        held,
        words,
        sem,
    )
    send_product(left_near_ref, right_near_ref, words.at[0], chosen, product, two_ref)

    @pl.when(odd)
    def _():
        send_product(left_far_ref, right_near_ref, words.at[1], chosen, product, three_ref)

    @pl.when(jnp.logical_not(odd))
    def _():
        send_product(left_own_ref, right_near_ref, words.at[1], chosen, product, three_ref)


def final_kernel(
    base_ref, two_factor, three_factor, scale, two_ref, three_ref, density_ref, term_out, density_out
):
    two = two_factor[...] * two_ref[...].astype(jnp.float32)
    three = three_factor[...] * three_ref[...].astype(jnp.float32)
    term_next = (base_ref[...] + (two + three)).astype(jnp.bfloat16)
    term_out[...] = term_next
    density_out[...] = density_ref[...] + scale[0:1, 0:1] * term_next.astype(jnp.float32)


ANYWHERE = pl.BlockSpec(memory_space=pl.ANY)
IN_VMEM = pl.BlockSpec(memory_space=pltpu.VMEM)
IN_SMEM = pl.BlockSpec(memory_space=pltpu.SMEM)
PANEL = (WB * BS, WB * BS)
RESULT = jax.ShapeDtypeStruct(PANEL, jnp.float32)
SENT = jax.ShapeDtypeStruct(PANEL, jnp.bfloat16)
LISTS = [
    pltpu.VMEM((8, LANES), jnp.int32),
    pltpu.SMEM((8, LANES), jnp.int32),
    pltpu.SMEM((LANES,), jnp.int32),
    pltpu.SemaphoreType.DMA,
]


def run_kernel(kernel, in_specs, out_shape, scratch_shapes, products, *args):
    return pl.pallas_call(
        kernel,
        out_shape=out_shape,
        in_specs=in_specs,
        out_specs=[IN_VMEM] * len(out_shape),
        scratch_shapes=scratch_shapes,
        compiler_params=pltpu.CompilerParams(vmem_limit_bytes=KERNEL_VMEM),
        cost_estimate=pl.CostEstimate(
            flops=products * 2 * WB * WB * BS * BS * BS * 40,
            bytes_accessed=4 * len(out_shape) * WB * WB * BS * BS,
            transcendentals=0,
        ),
    )(*args)


def per_device(
    hamiltonian,
    term_now,
    hamiltonian_ids,
    term_ids,
    product_filter,
    term_before,
    density_in,
    coefficient,
):
    left_own, right_own = gather_blocks(hamiltonian, term_now, hamiltonian_ids, term_ids)
    left_n = move(left_own, left_near)
    right_f = move(right_own, right_far)
    right_n = move(right_own, right_near)
    left_f = move(left_own, left_far)

    def in_vmem(panel):
        return pltpu.with_memory_space_constraint(panel, pltpu.VMEM)

    (own,) = run_kernel(
        own_kernel,
        [IN_VMEM] * 2,
        [RESULT],
        LISTS,
        1,
        in_vmem(left_own),
        in_vmem(right_own),
    )
    (one,) = run_kernel(
        early_kernel,
        [ANYWHERE] + [IN_VMEM] * 3,
        [SENT],
        [pltpu.VMEM(PANEL, jnp.float32)] + LISTS,
        1,
        own,
        *[in_vmem(panel) for panel in (left_n, right_f, right_own)],
    )
    two, three = run_kernel(
        late_kernel,
        [ANYWHERE] + [IN_VMEM] * 4,
        [SENT] * 2,
        [pltpu.VMEM(PANEL, jnp.float32)] + LISTS,
        2,
        one,
        *[in_vmem(panel) for panel in (left_n, right_n, left_f, left_own)],
    )
    two, three, one = move(two, home_two), move(three, home_three), move(one, home_one)
    base, two_factor, three_factor, scale = run_kernel(
        base_kernel,
        [IN_SMEM] * 2 + [IN_VMEM] * 3,
        [RESULT] * 3 + [jax.ShapeDtypeStruct((8, LANES), jnp.float32)],
        [],
        0,
        product_filter,
        coefficient,
        own,
        one,
        term_before,
    )
    term_next, density_out = run_kernel(
        final_kernel,
        [IN_VMEM] * 7,
        [
            jax.ShapeDtypeStruct(term_before.shape, jnp.bfloat16),
            jax.ShapeDtypeStruct(density_in.shape, jnp.float32),
        ],
        [],
        0,
        base,
        two_factor,
        three_factor,
        scale,
        two,
        three,
        density_in,
    )
    return (term_next, density_out)


def solution(mesh):
    return jax.shard_map(
        per_device,
        mesh=mesh,
        in_specs=(
            P("row", "col"),
            P("row", "col"),
            P("row", "col", None),
            P("row", "col", None),
            P(None, "row", "col"),
            P("row", "col"),
            P("row", "col"),
            P(),
        ),
        out_specs=(P("row", "col"), P("row", "col")),
        check_vma=False,
    )
```
